32 devices in a mesh: tile: 2 (over core), view: 16 (over z, y, x).
Axes of the slice: x: 2, y: 2, z: 4, core: 2. Of those that a mesh axis runs over, the one named last changes fastest.
Arguments:
- estimate: float32 [48, 768, 128], P('tile', 'view'), may hold values from 0.5 to 1.5
- views: float32 [6, 48, 768, 128], P(None, 'tile', 'view'), may hold values from 0.1 to 3
- background: float32 [6], replicated, may hold values from 0.1 to 1
- psf_taps: float32 [6, 3, 11], replicated, may hold values from 0.2 to 1
- psf_lengths: int32 [6, 3], replicated, may hold values from 3 to 11, as said below
- view_offsets: int32 [6, 3], replicated, may hold values from -4 to 4, as said below
- field_rows: int32 [6, 2], replicated, may hold values from 0 to 768, as said below
Outputs:
- restored: float32 [48, 768, 128], P('tile', 'view')
The draws below stay inside these ranges and needn't reach their ends.
Inputs may be any that keep to these rules, and one draw needn't show every extreme that they name: `psf_lengths`: odd; for each dimension some view has length 11. `view_offsets`: for each dimension some view has offset 4 and another -4. `field_rows`: the first column is at most 192 and the second at least 576; some view starts at row 0 and some ends at row 768.
All inputs are finite; a program needn't handle non-finite values.
Results may differ from the reference program's by a relative error of at most 0.0003.
Values sent between devices are 32-bit elements; how exact they have to be, the bound alone decides.
No kernel may reach another device: no remote copies, remote signals or barrier semaphores. Data moves between devices by JAX's collectives and lax.ppermute only.
A program may use at most 64 MiB of HBM per device.

```python
import math
import jax
import jax.numpy as jnp
from jax import lax

VIEWS = 6
KMAX = 11
OFF = 4
LANES = 128
ITERS = 2
HALO = 9
NZ = 48
NY = 768


def draw_psf_lengths(key, part):
    first_key, second_key = jax.random.split(jax.random.fold_in(key, 11))
    halves = jax.random.randint(first_key, (VIEWS, 3), 1, KMAX // 2 + 1)
    chosen = jax.random.randint(second_key, (3,), 0, VIEWS)
    halves = halves.at[chosen, jnp.arange(3)].set(KMAX // 2)
    return (2 * halves + 1).astype(jnp.int32)


def draw_view_offsets(key, part):
    first_key, second_key = jax.random.split(jax.random.fold_in(key, 23))
    shifts = jax.random.randint(first_key, (VIEWS, 3), -OFF, OFF + 1)
    order = jax.vmap(lambda item: jax.random.permutation(item, VIEWS))(jax.random.split(second_key, 3))
    shifts = shifts.at[order[:, 0], jnp.arange(3)].set(OFF)
    shifts = shifts.at[order[:, 1], jnp.arange(3)].set(-OFF)
    return shifts.astype(jnp.int32)


def draw_field_rows(key, part):
    first_key, second_key, third_key = jax.random.split(jax.random.fold_in(key, 37), 3)
    quarter = NY // 4
    lower = jax.random.randint(first_key, (VIEWS,), 0, quarter + 1)
    upper = NY - jax.random.randint(second_key, (VIEWS,), 0, quarter + 1)
    order = jax.random.permutation(third_key, VIEWS)
    lower = lower.at[order[0]].set(0)
    upper = upper.at[order[1]].set(NY)
    return jnp.stack([lower, upper], axis=1).astype(jnp.int32)


def levels(key, dims, shards, low, high):
    level, own = 1.0, jax.random.fold_in(key, 6)
    for axis_at, shards_of in shards:
        draws = jnp.exp(jax.random.uniform(jax.random.fold_in(own, axis_at), (shards_of,), jnp.float32, low / len(shards), high / len(shards)))
        level = level * jnp.repeat(draws, dims[axis_at] // shards_of).reshape([-1 if axis == axis_at else 1 for axis in range(len(dims))])
    return level


def setup_inputs(seed: int = 0) -> dict:
    splits = jax.random.split(jax.random.key(seed), 8)
    estimate = jnp.clip(0.5 + 1.0 * jax.random.uniform(splits[0], (NZ, NY, LANES), jnp.float32) ** levels(splits[0], (NZ, NY, LANES), ((0, 2), (1, 16)), -0.2, 0.2), 0.5, 1.5)
    views = jnp.clip(jnp.exp(math.log(3.0) - 3.4011974 * jax.random.uniform(splits[1], (VIEWS, NZ, NY, LANES), jnp.float32) ** levels(splits[1], (VIEWS, NZ, NY, LANES), ((1, 2), (2, 16)), -0.2, 0.2)), 0.1, 3.0)
    background = jnp.clip(jnp.exp(jax.random.uniform(splits[2], (VIEWS,), jnp.float32, math.log(0.1), math.log(1.0))), 0.1, 1.0)
    psf_taps = jnp.clip(jax.random.uniform(splits[3], (VIEWS, 3, KMAX), jnp.float32, 0.2, 1.0), 0.2, 1.0)
    psf_lengths = draw_psf_lengths(jax.random.fold_in(splits[7], 71), 0)
    view_offsets = draw_view_offsets(jax.random.fold_in(splits[7], 71), 0)
    field_rows = draw_field_rows(jax.random.fold_in(splits[7], 71), 0)
    return dict(estimate=estimate, views=views, background=background, psf_taps=psf_taps, psf_lengths=psf_lengths, view_offsets=view_offsets, field_rows=field_rows)


def taps_table(psf_taps, psf_lengths):
    places = jnp.arange(KMAX, dtype=jnp.int32)
    live = (places[None, None, :] < psf_lengths[:, :, None]).astype(psf_taps.dtype)
    raw = psf_taps * live
    return raw / jnp.sum(raw, axis=2, keepdims=True)


def slide(field, weights, start, axis, sign):
    size = field.shape[axis]
    widths = [(0, 0), (0, 0), (0, 0)]
    widths[axis] = (HALO, HALO)
    padded = jnp.pad(field, widths)
    total = jnp.zeros_like(field)
    for place in range(KMAX):
        begin = (HALO + sign * (start + place)).astype(jnp.int32)
        total = total + weights[place] * lax.dynamic_slice_in_dim(padded, begin, size, axis)
    return total


def reference(estimate, views, background, psf_taps, psf_lengths, view_offsets, field_rows):
    weights = taps_table(psf_taps, psf_lengths)
    start = (view_offsets - psf_lengths // 2).astype(jnp.int32)
    places = jnp.arange(estimate.shape[1], dtype=jnp.int32)
    restored = estimate
    for step in range(ITERS):
        def one_view(total, item):
            observed, level, kernel, begin, bounds = item
            blurred = restored
            for axis in range(3):
                blurred = slide(blurred, kernel[axis], begin[axis], axis, 1)
            covered = (places >= bounds[0]) & (places < bounds[1])
            ratio = jnp.where(covered[None, :, None], observed / (blurred + level), 1.0)
            spread = ratio
            for axis in range(3):
                spread = slide(spread, kernel[axis], begin[axis], axis, -1)
            return total + spread, None

        total, unused = lax.scan(one_view, jnp.zeros_like(restored), (views, background, weights, start, field_rows))
        restored = restored * total / VIEWS
    return restored
```

```python
import functools

import jax
import jax.numpy as jnp
from jax import lax
from jax.experimental import pallas as pl
from jax.experimental.pallas import tpu as pltpu
from jax.sharding import PartitionSpec as P

ITERS = 2
HALO = 9
FAR = 1 << 20
F32 = jnp.float32
BF16 = jnp.bfloat16


def up(size, unit):
    return -(-size // unit) * unit


class Plan:
    def __init__(self, views, depth, rows, lanes, tiles):
        self.views, self.depth, self.rows, self.lanes = views, depth, rows, lanes
        self.z_stages = 1 if tiles == 2 else 2
        self.z_side = up(HALO, 8)
        self.z_used = depth + self.z_side * self.z_stages
        self.z_slots = up(self.z_used, 16)
        self.y_used = rows + 2 * HALO
        self.y_slots = up(self.y_used, 16)
        self.pitch = self.y_slots + (8 if (self.y_slots // 8) % 2 == 0 else 0)
        self.stack = views * depth


def swaps(count):
    first, second = [], []
    for i in range(0, count - 1, 2):
        first += [(i, i + 1), (i + 1, i)]
    for i in range(1, count - 1, 2):
        second += [(i, i + 1), (i + 1, i)]
    return first, second


def split(value):
    high = value.astype(BF16)
    return high, (value - high.astype(F32)).astype(BF16)


def place(slot, own, side, stages, even):
    after, before = slot, slot - own - side
    first = jnp.where(even == 1, after, before)
    second = jnp.where(even == 1, before - side, after - side)
    far = jnp.full_like(slot, FAR)
    last = jnp.where(slot < own + 2 * side, second, far) if stages == 2 else far
    return jnp.where(slot < own, slot, jnp.where(slot < own + side, first, last))


def bands_kernel(plan, where_ref, start_ref, taps_ref, zf_ref, za_ref, yf_ref, ya_ref, xf_ref, xa_ref, zf_wide):
    views, depth, rows, lanes = plan.views, plan.depth, plan.rows, plan.lanes
    taps = taps_ref.shape[0] // (views * 3)
    even_z, even_y = where_ref[0], where_ref[1]

    def weight(v, d, k):
        return taps_ref[(v * 3 + d) * taps + k]

    def banded(v, d, delta):
        value = jnp.zeros(delta.shape, F32)
        for k in range(taps):
            value = jnp.where(delta == k, weight(v, d, k), value)
        return value

    def parted(value, low):
        high = value.astype(BF16).astype(F32)
        return jnp.where(low, value - high, high)

    def columns(count, period):
        column = lax.broadcasted_iota(jnp.int32, (1, count * period), 1)
        part = jnp.zeros_like(column)
        for i in range(1, count):
            part = part + (column >= i * period).astype(jnp.int32)
        return part, column - part * period

    part, slot = columns(3, plan.z_slots)
    z_in = place(slot, depth, plan.z_side, plan.z_stages, even_z)
    z_out = lax.broadcasted_iota(jnp.int32, (depth, 1), 0)
    for v in range(views):
        value = banded(v, 0, z_in - z_out - start_ref[v * 3])
        zf_wide[v * depth : (v + 1) * depth, :] = parted(value, part == 2)
    zf_ref[...] = zf_wide[...].astype(BF16)

    part, column = columns(3, plan.stack)
    view = jnp.zeros_like(column)
    for v in range(1, views):
        view = view + (column >= v * depth).astype(jnp.int32)
    begin = jnp.zeros_like(column)
    for v in range(views):
        begin = jnp.where(view == v, start_ref[v * 3], begin)
    z_in = column - view * depth
    slot = lax.broadcasted_iota(jnp.int32, (plan.z_slots, 1), 0)
    z_out = place(slot, depth, plan.z_side, plan.z_stages, even_z)
    delta = z_out - (z_in + begin)
    value = jnp.zeros(delta.shape, F32)
    for k in range(taps):
        row = jnp.zeros(column.shape, F32)
        for v in range(views):
            row = jnp.where(view == v, weight(v, 0, k), row)
        value = jnp.where(delta == k, row, value)
    za_ref[...] = parted(value, part == 2).astype(BF16)

    def of_view(v, carry):
        part, slot = columns(3, plan.y_slots)
        y_in = place(slot, rows, HALO, 2, even_y)
        y_out = lax.broadcasted_iota(jnp.int32, (rows, 1), 0)
        value = banded(v, 1, y_in - y_out - start_ref[v * 3 + 1])
        yf_ref[v] = parted(value, part == 2).astype(BF16)

        part, y_in = columns(3, rows)
        slot = lax.broadcasted_iota(jnp.int32, (plan.y_slots, 1), 0)
        y_out = place(slot, rows, HALO, 2, even_y)
        value = banded(v, 1, y_out - y_in - start_ref[v * 3 + 1])
        ya_ref[v] = parted(value, part == 2).astype(BF16)

        x_in = lax.broadcasted_iota(jnp.int32, (lanes, lanes), 0)
        x_out = lax.broadcasted_iota(jnp.int32, (lanes, lanes), 1)
        for ref, delta in ((xf_ref, x_in - x_out), (xa_ref, x_out - x_in)):
            high, low = split(banded(v, 2, delta - start_ref[v * 3 + 2]))
            ref[v, :, :lanes] = high
            ref[v, :, lanes:] = low
        return carry

    lax.fori_loop(0, views, of_view, 0)


def bands(plan, where, start, taps):
    views, lanes = plan.views, plan.lanes
    shapes = (
        (plan.stack, 3 * plan.z_slots),
        (plan.z_slots, 3 * plan.stack),
        (views, plan.rows, 3 * plan.y_slots),
        (views, plan.y_slots, 3 * plan.rows),
        (views, lanes, 2 * lanes),
        (views, lanes, 2 * lanes),
    )
    smem = pl.BlockSpec(memory_space=pltpu.SMEM)
    vmem = pl.BlockSpec(memory_space=pltpu.VMEM)
    return pl.pallas_call(
        functools.partial(bands_kernel, plan),
        out_shape=[jax.ShapeDtypeStruct(shape, BF16) for shape in shapes],
        in_specs=[smem] * 3,
        out_specs=[vmem] * len(shapes),
        scratch_shapes=[pltpu.VMEM(shapes[0], F32)],
        compiler_params=pltpu.CompilerParams(vmem_limit_bytes=24 << 20),
        cost_estimate=pl.CostEstimate(flops=10_000_000, bytes_accessed=4_000_000, transcendentals=0),
        name="bands",
    )(where, start, taps)


def dot(a, b):
    return jnp.dot(a, b, preferred_element_type=F32)


def step_kernel(
    plan, where_ref, field_ref, level_ref, own_ref, side_ref, zf_ref, za_ref, yf_ref, ya_ref, xf_ref, xa_ref, views_hbm,
    own_out, side_out, grid_ref, views_ref, sems,
):
    views, depth, rows, lanes = plan.views, plan.depth, plan.rows, plan.lanes
    pitch, y_slots, stack = plan.pitch, plan.y_slots, plan.stack
    sides = plan.z_used - depth

    def fetch(v):
        return pltpu.make_async_copy(views_hbm.at[v], views_ref.at[v], sems.at[v])

    for v in range(views):
        fetch(v).start()

    blank = jnp.zeros((y_slots - plan.y_used // 8 * 8, lanes), F32)

    def clear(i, carry):
        grid_ref[pl.ds(i * pitch + plan.y_used // 8 * 8, blank.shape[0]), :] = blank
        return carry

    lax.fori_loop(0, stack, clear, 0, unroll=8)

    def three(value):
        high, low = split(value)
        return jnp.concatenate([high, low, high], axis=0)

    def z_forward(pair, carry):
        parts = []
        for i in range(2):
            y = pair * 2 + i
            pieces = [own_ref[y], side_ref[y]]
            if plan.z_slots > plan.z_used:
                pieces.append(jnp.zeros((plan.z_slots - plan.z_used, lanes), F32))
            parts.append(three(jnp.concatenate(pieces, axis=0)))
        out = dot(zf_ref[...], jnp.concatenate(parts, axis=1))
        for i in range(2):
            grid_ref[pl.ds(pair * 2 + i, stack, stride=pitch), :] = out[:, i * lanes : (i + 1) * lanes]
        return carry

    lax.fori_loop(0, plan.y_used // 2, z_forward, 0, unroll=3)

    def of_view(v, carry):
        fetch(v).wait()
        lower, upper, first = field_ref[v * 2], field_ref[v * 2 + 1], where_ref[2]
        level = level_ref[v]
        y = first + lax.broadcasted_iota(jnp.int32, (rows, lanes), 0)
        covered = (y >= lower) & (y < upper)
        lane_forward = jnp.concatenate([xf_ref[v]] * 2, axis=0)
        lane_adjoint = jnp.concatenate([xa_ref[v]] * 2, axis=0)

        def along_x(value, matrix):
            out = dot(jnp.concatenate(split(value), axis=1), matrix)
            return out[:, :lanes] + out[:, lanes:]

        chunk = 8
        for z0 in range(0, depth, chunk):
            base = pl.multiple_of((v * depth + z0) * pitch, 8)
            spread = []
            for z in range(0, chunk, 2):
                parts = [three(grid_ref[pl.ds(base + (z + i) * pitch, y_slots), :]) for i in range(2)]
                out = dot(yf_ref[v], jnp.concatenate(parts, axis=1))
                spread += [out[:, :lanes], out[:, lanes:]]
            blurred = along_x(jnp.concatenate(spread, axis=0), lane_forward).reshape(chunk, rows, lanes)
            ratio = jnp.where(covered[None], views_ref[v, z0 : z0 + chunk] / (blurred + level), 1.0)
            back = along_x(ratio.reshape(chunk * rows, lanes), lane_adjoint)
            for z in range(0, chunk, 2):
                parts = [three(back[(z + i) * rows : (z + i + 1) * rows]) for i in range(2)]
                out = dot(ya_ref[v], jnp.concatenate(parts, axis=1))
                for i in range(2):
                    grid_ref[pl.ds(base + (z + i) * pitch, y_slots), :] = out[:, i * lanes : (i + 1) * lanes]
        return carry

    lax.fori_loop(0, views, of_view, 0)

    def z_adjoint(pair, carry):
        parts = [three(grid_ref[pl.ds(pair * 2 + i, stack, stride=pitch), :]) for i in range(2)]
        out = dot(za_ref[...], jnp.concatenate(parts, axis=1))
        for i in range(2):
            value = out[:, i * lanes : (i + 1) * lanes]
            own_out[pair * 2 + i] = value[:depth]
            side_out[pair * 2 + i] = value[depth : depth + sides]
        return carry

    lax.fori_loop(0, plan.y_used // 2, z_adjoint, 0, unroll=3)


def step(plan, where, field, level, own, side, tables, views):
    smem = pl.BlockSpec(memory_space=pltpu.SMEM)
    vmem = pl.BlockSpec(memory_space=pltpu.VMEM)
    sides = plan.z_used - plan.depth
    return pl.pallas_call(
        functools.partial(step_kernel, plan),
        out_shape=[
            jax.ShapeDtypeStruct((plan.y_used, plan.depth, plan.lanes), F32),
            jax.ShapeDtypeStruct((plan.y_used, sides, plan.lanes), F32),
        ],
        in_specs=[smem] * 3 + [vmem] * 8 + [pl.BlockSpec(memory_space=pl.ANY)],
        out_specs=[vmem] * 2,
        scratch_shapes=[
            pltpu.VMEM((plan.stack * plan.pitch, plan.lanes), F32),
            pltpu.VMEM(views.shape, F32),
            pltpu.SemaphoreType.DMA((plan.views,)),
        ],
        compiler_params=pltpu.CompilerParams(vmem_limit_bytes=40 << 20),
        cost_estimate=pl.CostEstimate(flops=8_000_000_000, bytes_accessed=8_000_000, transcendentals=0),
        name="step",
    )(where, field, level, own, side, *tables, views)


def taps_table(psf_taps, psf_lengths):
    places = jnp.arange(psf_taps.shape[2], dtype=jnp.int32)
    live = (places[None, None, :] < psf_lengths[:, :, None]).astype(jnp.float32)
    raw = psf_taps * live
    return raw / jnp.sum(raw, axis=2, keepdims=True)


def on_device(estimate, views, background, psf_taps, psf_lengths, view_offsets, field_rows):
    count = views.shape[0]
    depth, rows, lanes = estimate.shape
    tiles, blocks = lax.axis_size("tile"), lax.axis_size("view")
    plan = Plan(count, depth, rows, lanes, tiles)
    z_side, halo = plan.z_side, HALO
    tile_at, view_at = lax.axis_index("tile"), lax.axis_index("view")
    even_z, even_y = 1 - tile_at % 2, 1 - view_at % 2
    where = jnp.stack([even_z, even_y, view_at * rows]).astype(jnp.int32)
    weights = taps_table(psf_taps, psf_lengths).reshape(-1)
    start = (view_offsets - psf_lengths // 2).reshape(-1)
    field = field_rows.reshape(-1)
    z_pairs, y_pairs = swaps(tiles), swaps(blocks)

    z_near = [jnp.where(even_z == 1, depth - z_side, 0), jnp.where(even_z == 1, 0, depth - z_side)]
    y_near = [jnp.where(even_y == 1, rows - halo, 0), jnp.where(even_y == 1, 0, rows - halo)]

    def z_swap(values):
        return [lax.ppermute(value, "tile", pairs) for value, pairs in zip(values, z_pairs)]

    def y_swap(values):
        return [lax.ppermute(value, "view", pairs) for value, pairs in zip(values, y_pairs)]

    def z_slabs(value):
        return [lax.dynamic_slice_in_dim(value, at, z_side, 1) for at in z_near[: plan.z_stages]]

    def z_sum(own, side):
        sent = [side[:, i * z_side : (i + 1) * z_side] for i in range(plan.z_stages)]
        for got, at in zip(z_swap(sent), z_near):
            own = lax.dynamic_update_slice_in_dim(own, lax.dynamic_slice_in_dim(own, at, z_side, 1) + got, at, 1)
        return own

    def ends(value):
        return [value[rows : rows + halo], value[rows + halo :]]

    block = jnp.transpose(estimate, (1, 0, 2))
    got = y_swap([lax.dynamic_slice_in_dim(block, at, halo, 0) for at in y_near])
    own = jnp.concatenate([block] + got, axis=0)
    tables = bands(plan, where, start, weights)
    for turn in range(ITERS):
        side = jnp.concatenate(z_swap(z_slabs(own)), axis=1)
        summed, beyond = step(plan, where, field, background, own, side, tables, views)
        summed = z_sum(summed, beyond)
        if turn < ITERS - 1:
            near = [lax.dynamic_slice_in_dim(summed, at, halo, 0) for at in y_near]
            got = y_swap([jnp.concatenate([end, inner], axis=0) for end, inner in zip(ends(summed), near)])
            total = summed[:rows]
            for piece, inner, at in zip(got, near, y_near):
                total = lax.dynamic_update_slice_in_dim(total, inner + piece[:halo], at, 0)
            outer = [end + piece[halo:] for end, piece in zip(ends(summed), got)]
            own = own * jnp.concatenate([total] + outer, axis=0) / count
        else:
            got = y_swap(ends(summed))
            total = summed[:rows]
            for piece, at in zip(got, y_near):
                inner = lax.dynamic_slice_in_dim(total, at, halo, 0)
                total = lax.dynamic_update_slice_in_dim(total, inner + piece, at, 0)
            own = own[:rows] * total / count
    return jnp.transpose(own, (1, 0, 2))


def solution(mesh):
    in_specs = (P("tile", "view", None), P(None, "tile", "view", None), P(), P(), P(), P(), P())
    out_specs = P("tile", "view", None)
    return jax.shard_map(
        on_device, mesh=mesh, in_specs=in_specs, out_specs=out_specs, check_vma=False
    )
```

```python
import functools

import jax
import jax.numpy as jnp
from jax import lax
from jax.experimental import pallas as pl
from jax.experimental.pallas import tpu as pltpu
from jax.sharding import PartitionSpec as P

ITERS = 2
HALO = 9
FAR = 1 << 20
UNROLL = 11
F32 = jnp.float32
BF16 = jnp.bfloat16


def up(size, unit):
    return -(-size // unit) * unit


class Plan:
    def __init__(self, views, taps, depth, rows, lanes, tiles):
        self.views, self.taps, self.depth, self.rows, self.lanes = views, taps, depth, rows, lanes
        self.z_stages = 1 if tiles == 2 else 2
        self.z_side = up(HALO, 8)
        self.z_used = depth + self.z_side * self.z_stages
        self.z_slots = up(self.z_used, 16)
        self.y_edge = 4 * HALO
        self.y_used = rows + 2 * HALO
        self.y_slots = up(self.y_used, 16)
        self.pitch = self.y_slots + (8 if (self.y_slots // 8) % 2 == 0 else 0)
        self.stack = views * depth

    def length_at(self, v, d):
        return 3 + v * 3 + d

    def offset_at(self, v, d):
        return 3 + self.views * 3 + v * 3 + d

    def field_at(self, v, end):
        return 3 + self.views * 6 + v * 2 + end

    def tap_at(self, v, d, k):
        return self.views + (v * 3 + d) * self.taps + k


def swaps(count):
    first, second = [], []
    for i in range(0, count - 1, 2):
        first += [(i, i + 1), (i + 1, i)]
    for i in range(1, count - 1, 2):
        second += [(i, i + 1), (i + 1, i)]
    return first, second


def split(value):
    high = value.astype(BF16)
    return high, (value - high.astype(F32)).astype(BF16)


def three(value):
    high, low = split(value)
    return jnp.concatenate([high, low, high], axis=0)


def dot(a, b):
    return jnp.dot(a, b, preferred_element_type=F32)


def z_place(plan, slot, even):
    own, side = plan.depth, plan.z_side
    after, before = slot, slot - own - side
    first = jnp.where(even == 1, after, before)
    second = jnp.where(even == 1, before - side, after - side)
    far = jnp.full_like(slot, FAR)
    last = jnp.where(slot < own + 2 * side, second, far) if plan.z_stages == 2 else far
    return jnp.where(slot < own, slot, jnp.where(slot < own + side, first, last))


def y_first_rows(plan, even):
    rows = plan.rows
    return [
        jnp.where(even == 1, rows, -HALO),
        jnp.where(even == 1, -HALO, rows),
        jnp.where(even == 1, rows - HALO, 0),
        jnp.where(even == 1, 0, rows - HALO),
        HALO,
    ]


def y_place(plan, slot, even):
    place = jnp.full_like(slot, FAR)
    begins = [0, HALO, 2 * HALO, 3 * HALO, 4 * HALO, plan.y_used]
    for begin, end, row in zip(begins, begins[1:], y_first_rows(plan, even)):
        place = jnp.where((slot >= begin) & (slot < end), slot - begin + row, place)
    return place


def bands_kernel(plan, ints, floats, zf_ref, za_ref, yf_ref, ya_ref, xf_ref, xa_ref, zf_wide):
    views, depth, rows, lanes, taps = plan.views, plan.depth, plan.rows, plan.lanes, plan.taps
    even_z, even_y = ints[0], ints[1]

    def start(v, d):
        return ints[plan.offset_at(v, d)] - ints[plan.length_at(v, d)] // 2

    def kernel(v, d):
        length = ints[plan.length_at(v, d)]
        raw = [jnp.where(k < length, floats[plan.tap_at(v, d, k)], 0.0) for k in range(taps)]
        total = raw[0]
        for one in raw[1:]:
            total = total + one
        return raw, 1.0 / jnp.full((1, lanes), total, F32)[:, :1]

    def banded(v, d, delta):
        raw, scale = kernel(v, d)
        value = jnp.zeros(delta.shape, F32)
        for k in range(taps):
            value = jnp.where(delta == k, raw[k], value)
        return value * scale

    def parted(value, low):
        high = value.astype(BF16).astype(F32)
        return jnp.where(low, value - high, high)

    def columns(count, period):
        column = lax.broadcasted_iota(jnp.int32, (1, count * period), 1)
        part = jnp.zeros_like(column)
        for i in range(1, count):
            part = part + (column >= i * period).astype(jnp.int32)
        return part, column - part * period

    part, slot = columns(3, plan.z_slots)
    z_in = z_place(plan, slot, even_z)
    z_out = lax.broadcasted_iota(jnp.int32, (depth, 1), 0)
    for v in range(views):
        value = banded(v, 0, z_in - z_out - start(v, 0))
        zf_wide[v * depth : (v + 1) * depth, :] = parted(value, part == 2)
    zf_ref[...] = zf_wide[...].astype(BF16)

    part, column = columns(3, plan.stack)
    view = jnp.zeros_like(column)
    for v in range(1, views):
        view = view + (column >= v * depth).astype(jnp.int32)
    begin = jnp.zeros_like(column)
    for v in range(views):
        begin = jnp.where(view == v, start(v, 0), begin)
    slot = lax.broadcasted_iota(jnp.int32, (plan.z_slots, 1), 0)
    delta = z_place(plan, slot, even_z) - (column - view * depth + begin)
    kernels = [kernel(v, 0) for v in range(views)]
    value = jnp.zeros(delta.shape, F32)
    for k in range(taps):
        row = jnp.zeros(column.shape, F32)
        for v in range(views):
            row = jnp.where(view == v, kernels[v][0][k] * kernels[v][1], row)
        value = jnp.where(delta == k, row, value)
    za_ref[...] = parted(value, part == 2).astype(BF16)

    def of_view(v, carry):
        part, slot = columns(3, plan.y_slots)
        y_out = lax.broadcasted_iota(jnp.int32, (rows, 1), 0)
        value = banded(v, 1, y_place(plan, slot, even_y) - y_out - start(v, 1))
        yf_ref[v] = parted(value, part == 2).astype(BF16)

        part, y_in = columns(3, rows)
        slot = lax.broadcasted_iota(jnp.int32, (plan.y_slots, 1), 0)
        value = banded(v, 1, y_place(plan, slot, even_y) - y_in - start(v, 1))
        ya_ref[v] = parted(value, part == 2).astype(BF16)

        x_in = lax.broadcasted_iota(jnp.int32, (lanes, lanes), 0)
        x_out = lax.broadcasted_iota(jnp.int32, (lanes, lanes), 1)
        for ref, delta in ((xf_ref, x_in - x_out), (xa_ref, x_out - x_in)):
            high, low = split(banded(v, 2, delta - start(v, 2)))
            ref[v, :, :lanes] = high
            ref[v, :, lanes:] = low
        return carry

    lax.fori_loop(0, views, of_view, 0)


SMEM = pl.BlockSpec(memory_space=pltpu.SMEM)
VMEM = pl.BlockSpec(memory_space=pltpu.VMEM)


def call(body, name, operands, specs, shapes, scratch=(), megabytes=16, flops=1_000_000):
    return pl.pallas_call(
        body,
        out_shape=[jax.ShapeDtypeStruct(*shape) for shape in shapes],
        in_specs=specs,
        out_specs=[VMEM] * len(shapes),
        scratch_shapes=list(scratch),
        compiler_params=pltpu.CompilerParams(vmem_limit_bytes=megabytes << 20),
        cost_estimate=pl.CostEstimate(flops=flops, bytes_accessed=2_000_000, transcendentals=0),
        name=name,
    )(*operands)


def bands(plan, ints, floats):
    views, lanes = plan.views, plan.lanes
    shapes = (
        (plan.stack, 3 * plan.z_slots),
        (plan.z_slots, 3 * plan.stack),
        (views, plan.rows, 3 * plan.y_slots),
        (views, plan.y_slots, 3 * plan.rows),
        (views, lanes, 2 * lanes),
        (views, lanes, 2 * lanes),
    )
    return call(
        functools.partial(bands_kernel, plan), "bands", (ints, floats), [SMEM] * 2, [(shape, BF16) for shape in shapes],
        scratch=[pltpu.VMEM(shapes[0], F32)], flops=2_000_000_000,
    )


def loop(count, body):
    unroll = max(d for d in range(1, UNROLL + 1) if count % d == 0)

    def run(i, carry):
        body(i)
        return carry

    lax.fori_loop(0, count, run, 0, unroll=unroll)


def z_forward(plan, own_ref, side_ref, zf_ref, grid_ref, first, count):
    lanes = plan.lanes

    def pair(at):
        parts = []
        for i in range(2):
            y = first + at * 2 + i
            pieces = [own_ref[y], side_ref[y]]
            if plan.z_slots > plan.z_used:
                pieces.append(jnp.zeros((plan.z_slots - plan.z_used, lanes), F32))
            parts.append(three(jnp.concatenate(pieces, axis=0)))
        out = dot(zf_ref[...], jnp.concatenate(parts, axis=1))
        for i in range(2):
            y = first + at * 2 + i
            grid_ref[pl.ds(y, plan.stack, stride=plan.pitch), :] = out[:, i * lanes : (i + 1) * lanes]

    loop(count // 2, pair)


def z_adjoint(plan, grid_ref, za_ref, own_out, side_out, first, count):
    lanes, depth = plan.lanes, plan.depth

    def pair(at):
        parts = [three(grid_ref[pl.ds(first + at * 2 + i, plan.stack, stride=plan.pitch), :]) for i in range(2)]
        out = dot(za_ref[...], jnp.concatenate(parts, axis=1))
        for i in range(2):
            value = out[:, i * lanes : (i + 1) * lanes]
            own_out[at * 2 + i] = value[:depth]
            side_out[at * 2 + i] = value[depth : plan.z_used]

    loop(count // 2, pair)


def clear_rest(plan, grid_ref):
    begin = plan.y_used // 8 * 8
    blank = jnp.zeros((plan.y_slots - begin, plan.lanes), F32)

    def one(i):
        grid_ref[pl.ds(i * plan.pitch + begin, blank.shape[0]), :] = blank

    loop(plan.stack, one)


def of_views(plan, ints, floats, yf_ref, ya_ref, xf_ref, xa_ref, views_ref, grid_ref, arrived):
    views, depth, rows, lanes = plan.views, plan.depth, plan.rows, plan.lanes
    pitch, y_slots = plan.pitch, plan.y_slots

    def of_view(v, carry):
        arrived(v)
        lower, upper = ints[plan.field_at(v, 0)], ints[plan.field_at(v, 1)]
        y = ints[2] + lax.broadcasted_iota(jnp.int32, (rows, lanes), 0)
        covered = (y >= lower) & (y < upper)
        lane_forward = jnp.concatenate([xf_ref[v]] * 2, axis=0)
        lane_adjoint = jnp.concatenate([xa_ref[v]] * 2, axis=0)

        def along_x(value, matrix):
            out = dot(jnp.concatenate(split(value), axis=1), matrix)
            return out[:, :lanes] + out[:, lanes:]

        base = pl.multiple_of(v * depth * pitch, 8)
        spread = []
        for z in range(0, depth, 2):
            parts = [three(grid_ref[pl.ds(base + (z + i) * pitch, y_slots), :]) for i in range(2)]
            out = dot(yf_ref[v], jnp.concatenate(parts, axis=1))
            spread += [out[:, :lanes], out[:, lanes:]]
        blurred = along_x(jnp.concatenate(spread, axis=0), lane_forward).reshape(depth, rows, lanes)
        ratio = jnp.where(covered[None], views_ref[v] / (blurred + floats[v]), 1.0)
        back = along_x(ratio.reshape(depth * rows, lanes), lane_adjoint)
        for z in range(0, depth, 2):
            parts = [three(back[(z + i) * rows : (z + i + 1) * rows]) for i in range(2)]
            out = dot(ya_ref[v], jnp.concatenate(parts, axis=1))
            for i in range(2):
                grid_ref[pl.ds(base + (z + i) * pitch, y_slots), :] = out[:, i * lanes : (i + 1) * lanes]
        return carry

    lax.fori_loop(0, views, of_view, 0)


def start_views(plan, views_hbm, views_ref, sems):
    def fetch(v):
        return pltpu.make_async_copy(views_hbm.at[v], views_ref.at[v], sems.at[v])

    for v in range(plan.views):
        fetch(v).start()
    return lambda v: fetch(v).wait()


def step_kernel(
    plan, ints, floats, own_ref, side_ref, zf_ref, za_ref, yf_ref, ya_ref, xf_ref, xa_ref, views_hbm, own_out, side_out,
    grid_ref, views_ref, sems,
):
    arrived = start_views(plan, views_hbm, views_ref, sems)
    clear_rest(plan, grid_ref)
    z_forward(plan, own_ref, side_ref, zf_ref, grid_ref, 0, plan.y_used)
    of_views(plan, ints, floats, yf_ref, ya_ref, xf_ref, xa_ref, views_ref, grid_ref, arrived)
    z_adjoint(plan, grid_ref, za_ref, own_out, side_out, 0, plan.y_used)


def first_step_kernel(
    plan, ints, floats, block_ref, block_side_ref, first_ref, second_ref, corner_ref, zf_ref, za_ref, yf_ref, ya_ref, xf_ref, xa_ref,
    views_hbm, own_out, side_out, own_ref, grid_ref, side_ref, views_ref, sems,
):
    arrived = start_views(plan, views_hbm, views_ref, sems)
    clear_rest(plan, grid_ref)
    depth, rows, sides = plan.depth, plan.rows, plan.z_used - plan.depth
    own_ref[:HALO] = first_ref[...]
    own_ref[HALO : 2 * HALO] = second_ref[...]
    side_ref[: 2 * HALO] = corner_ref[...]
    begins = [2 * HALO, 3 * HALO, 4 * HALO, plan.y_used]
    for begin, end, row in zip(begins, begins[1:], y_first_rows(plan, ints[1])[2:]):
        for i in range(end - begin):
            own_ref[begin + i] = block_ref[pl.ds(row + i, depth, stride=rows), :]
            side_ref[begin + i] = block_side_ref[pl.ds(row + i, sides, stride=rows), :]
    z_forward(plan, own_ref, side_ref, zf_ref, grid_ref, 0, plan.y_used)
    of_views(plan, ints, floats, yf_ref, ya_ref, xf_ref, xa_ref, views_ref, grid_ref, arrived)
    z_adjoint(plan, grid_ref, za_ref, own_out, side_out, 0, plan.y_used)


HBM = pl.BlockSpec(memory_space=pltpu.HBM)


def step(plan, ints, floats, own, side, tables, views):
    lanes = plan.lanes
    first = isinstance(own, (list, tuple))
    operands = list(own) if first else [own, side]
    used = (plan.y_used, plan.depth, lanes)
    shapes = [(used, F32), ((plan.y_used, plan.z_used - plan.depth, lanes), F32)] + ([(used, F32)] if first else [])
    scratch = [pltpu.VMEM((plan.stack * plan.pitch, lanes), F32)]
    scratch += [pltpu.VMEM(shapes[1][0], F32)] if first else []
    scratch += [pltpu.VMEM(views.shape, F32), pltpu.SemaphoreType.DMA((plan.views,))]
    return call(
        functools.partial(first_step_kernel if first else step_kernel, plan), "first_step" if first else "step",
        (ints, floats, *operands, *tables, views), [SMEM] * 2 + [VMEM] * (len(operands) + len(tables)) + [HBM], shapes,
        scratch=scratch, megabytes=40, flops=8_000_000_000,
    )


def add_sides(plan, even_z, piece, got_refs, at, count):
    depth, side = plan.depth, plan.z_side
    value = piece
    near = [even_z == 1, even_z != 1]
    for ref, last in zip(got_refs, near):
        got = ref[at : at + count]
        blank = jnp.zeros((count, depth - side, plan.lanes), F32)
        value = value + jnp.where(last, jnp.concatenate([blank, got], axis=1), jnp.concatenate([got, blank], axis=1))
    return value


def sums_kernel(plan, own_halo, ints, summed_ref, *refs):
    got_refs, (out_ref, first_ref, second_ref) = refs[: plan.z_stages], refs[plan.z_stages :]
    for at in range(0, plan.y_used, HALO):
        count = min(HALO, plan.y_used - at)
        out_ref[at : at + count] = add_sides(plan, ints[0], summed_ref[at : at + count], got_refs, at, count)
    for ref, i in ((first_ref, 0), (second_ref, 1)):
        ref[:HALO] = out_ref[i * HALO : (i + 1) * HALO]
        if own_halo:
            ref[HALO:] = out_ref[(i + 2) * HALO : (i + 3) * HALO]


def sums(plan, own_halo, ints, summed, got):
    used, sent = (plan.y_used, plan.depth, plan.lanes), (HALO * (2 if own_halo else 1), plan.depth, plan.lanes)
    return call(
        functools.partial(sums_kernel, plan, own_halo), "sums", (ints, summed, *got), [SMEM] + [VMEM] * (1 + len(got)),
        [(used, F32), (sent, F32), (sent, F32)],
    )


def next_kernel(plan, ints, own_ref, summed_ref, first_ref, second_ref, out_ref, *side_refs):
    scale = 1.0 / plan.views
    for i, ref in ((0, first_ref), (1, second_ref)):
        a, b = i * HALO, (i + 2) * HALO
        out_ref[a : a + HALO] = own_ref[a : a + HALO] * (summed_ref[a : a + HALO] + ref[HALO:]) * scale
        out_ref[b : b + HALO] = own_ref[b : b + HALO] * (summed_ref[b : b + HALO] + ref[:HALO]) * scale
    rest = 4 * HALO
    out_ref[rest:] = own_ref[rest:] * summed_ref[rest:] * scale
    depth, side = plan.depth, plan.z_side
    for ref, last in zip(side_refs, (ints[0] == 1, ints[0] != 1)):
        ref[...] = jnp.where(last, out_ref[:, depth - side :], out_ref[:, :side])


def next_estimate(plan, ints, own, summed, got):
    used, side = (plan.y_used, plan.depth, plan.lanes), (plan.y_used, plan.z_side, plan.lanes)
    return call(
        functools.partial(next_kernel, plan), "next", (ints, own, summed, *got), [SMEM] + [VMEM] * 4,
        [(used, F32)] + [(side, F32)] * plan.z_stages,
    )


def last_kernel(plan, ints, own_ref, summed_ref, first_ref, second_ref, out_ref):
    scale = 1.0 / plan.views
    begins = [2 * HALO, 3 * HALO, 4 * HALO, plan.y_used]
    for begin, end, row, got in zip(begins, begins[1:], y_first_rows(plan, ints[1])[2:], (first_ref, second_ref, None)):
        for i in range(end - begin):
            total = summed_ref[begin + i]
            if got is not None:
                total = total + got[i]
            out_ref[pl.ds(row + i, plan.depth, stride=plan.rows), :] = own_ref[begin + i] * total * scale


def last_estimate(plan, ints, own, summed, got):
    shape = (plan.depth * plan.rows, plan.lanes)
    out = call(functools.partial(last_kernel, plan), "last", (ints, own, summed, *got), [SMEM] + [VMEM] * 4, [(shape, F32)])
    return out[0].reshape(plan.depth, plan.rows, plan.lanes)


def on_device(estimate, views, background, psf_taps, psf_lengths, view_offsets, field_rows):
    depth, rows, lanes = estimate.shape
    tiles, blocks = lax.axis_size("tile"), lax.axis_size("view")
    plan = Plan(views.shape[0], psf_taps.shape[2], depth, rows, lanes, tiles)
    side = plan.z_side
    tile_at, view_at = lax.axis_index("tile"), lax.axis_index("view")
    even_z, even_y = 1 - tile_at % 2, 1 - view_at % 2
    where = jnp.stack([even_z, even_y, view_at * rows]).astype(jnp.int32)
    ints = jnp.concatenate([where, psf_lengths.reshape(-1), view_offsets.reshape(-1), field_rows.reshape(-1)])
    floats = jnp.concatenate([background, psf_taps.reshape(-1)])
    z_pairs, y_pairs = swaps(tiles), swaps(blocks)

    def z_swap(values):
        return [lax.ppermute(value, "tile", pairs) for value, pairs in zip(values, z_pairs)]

    def y_swap(values):
        second = lax.ppermute(values[1], "view", y_pairs[1])
        return [lax.ppermute(values[0], "view", y_pairs[0]), second]

    near = [lax.dynamic_slice_in_dim(estimate, row, HALO, 1).transpose(1, 0, 2) for row in y_first_rows(plan, even_y)[2:4]]
    got = y_swap(near)
    z_near = [jnp.where(even_z == 1, depth - side, 0), jnp.where(even_z == 1, 0, depth - side)][: plan.z_stages]
    block_side = jnp.concatenate(z_swap([lax.dynamic_slice_in_dim(estimate, at, side, 0) for at in z_near]), axis=0)
    tables = bands(plan, ints, floats)
    halo = jnp.concatenate(got, axis=0)
    halo, tables = lax.optimization_barrier((halo, tables))
    corner = jnp.concatenate(z_swap([lax.dynamic_slice_in_dim(halo, at, side, 1) for at in z_near]), axis=1)
    own = (estimate.reshape(depth * rows, lanes), block_side.reshape(-1, lanes), *got, corner)
    summed, beyond, own = step(plan, ints, floats, own, None, tables, views)
    for turn in range(1, ITERS + 1):
        sent = [beyond[:, i * side : (i + 1) * side] for i in range(plan.z_stages)]
        summed, *ends = sums(plan, turn < ITERS, ints, summed, z_swap(sent))
        got = y_swap(ends)
        if turn == ITERS:
            return last_estimate(plan, ints, own, summed, got)
        own, *sent = next_estimate(plan, ints, own, summed, got)
        summed, beyond = step(plan, ints, floats, own, jnp.concatenate(z_swap(sent), axis=1), tables, views)


def solution(mesh):
    in_specs = (P("tile", "view", None), P(None, "tile", "view", None), P(), P(), P(), P(), P())
    out_specs = P("tile", "view", None)
    return jax.shard_map(
        on_device, mesh=mesh, in_specs=in_specs, out_specs=out_specs, check_vma=False
    )
```

```python
import functools

import jax
import jax.numpy as jnp
from jax import lax
from jax.experimental import pallas as pl
from jax.experimental.pallas import tpu as pltpu
from jax.sharding import PartitionSpec as P

ITERS = 2
HALO = 9
FAR = 1 << 20
UNROLL = 18
F32 = jnp.float32
BF16 = jnp.bfloat16


def up(size, unit):
    return -(-size // unit) * unit


def odd_tiles(count):
    return count + (8 if (count // 8) % 2 == 0 else 0)


class Plan:
    def __init__(self, views, taps, depth, rows, lanes, tiles):
        self.views, self.taps, self.depth, self.rows, self.lanes = views, taps, depth, rows, lanes
        self.z_stages = 1 if tiles == 2 else 2
        self.z_side = up(HALO, 8)
        self.z_used = depth + self.z_side * self.z_stages
        self.z_slots = up(self.z_used, 16)
        self.y_edge = 4 * HALO
        self.y_inner = rows - 2 * HALO
        self.edge_pad, self.inner_pad = up(self.y_edge, 8), up(self.y_inner, 8)
        self.y_slots = up(self.edge_pad + self.inner_pad, 16)
        self.edge_pitch, self.inner_pitch = odd_tiles(self.edge_pad), odd_tiles(self.inner_pad)
        self.stack = views * depth


def swaps(count):
    first, second = [], []
    for i in range(0, count - 1, 2):
        first += [(i, i + 1), (i + 1, i)]
    for i in range(1, count - 1, 2):
        second += [(i, i + 1), (i + 1, i)]
    return first, second


def split(value):
    high = value.astype(BF16)
    return high, (value - high.astype(F32)).astype(BF16)


def two(value):
    return jnp.concatenate(split(value), axis=0)


def three(value):
    high, low = split(value)
    return jnp.concatenate([high, low, high], axis=0)


def dot(a, b):
    return jnp.dot(a, b, preferred_element_type=F32)


def z_place(plan, slot, even):
    own, side = plan.depth, plan.z_side
    after, before = slot, slot - own - side
    first = jnp.where(even == 1, after, before)
    second = jnp.where(even == 1, before - side, after - side)
    far = jnp.full_like(slot, FAR)
    last = jnp.where(slot < own + 2 * side, second, far) if plan.z_stages == 2 else far
    return jnp.where(slot < own, slot, jnp.where(slot < own + side, first, last))


def y_first_rows(plan, even):
    rows = plan.rows
    return [
        jnp.where(even == 1, rows, -HALO),
        jnp.where(even == 1, -HALO, rows),
        jnp.where(even == 1, rows - HALO, 0),
        jnp.where(even == 1, 0, rows - HALO),
        HALO,
    ]


def y_place(plan, slot, even):
    place = jnp.full_like(slot, FAR)
    begins = [0, HALO, 2 * HALO, 3 * HALO, plan.edge_pad]
    ends = [HALO, 2 * HALO, 3 * HALO, 4 * HALO, plan.edge_pad + plan.y_inner]
    for begin, end, row in zip(begins, ends, y_first_rows(plan, even)):
        place = jnp.where((slot >= begin) & (slot < end), slot - begin + row, place)
    return place


def evens():
    return 1 - lax.axis_index("tile") % 2, 1 - lax.axis_index("view") % 2


def bands_kernel(
    plan, lengths_hbm, offsets_hbm, taps_hbm, zf_ref, za_ref, yf_ref, ya_ref, xf_ref, xa_ref, zf_wide, lengths, offsets, tap_table, sems,
):
    pairs = ((lengths_hbm, lengths), (offsets_hbm, offsets), (taps_hbm, tap_table))
    copies = [pltpu.make_async_copy(source, target, sems.at[i]) for i, (source, target) in enumerate(pairs)]
    for copy in copies:
        copy.start()
    for copy in copies:
        copy.wait()
    views, depth, rows, lanes, taps = plan.views, plan.depth, plan.rows, plan.lanes, plan.taps
    even_z, even_y = evens()

    def start(v, d):
        return offsets[d, v] - lengths[d, v] // 2

    def kernel(v, d):
        length = lengths[d, v]
        raw = [jnp.where(k < length, tap_table[v, d, k], 0.0) for k in range(taps)]
        total = raw[0]
        for one in raw[1:]:
            total = total + one
        return raw, 1.0 / jnp.full((1, lanes), total, F32)[:, :1]

    def banded(v, d, delta):
        raw, scale = kernel(v, d)
        value = jnp.zeros(delta.shape, F32)
        for k in range(taps):
            value = jnp.where(delta == k, raw[k], value)
        return value * scale

    def parted(value, low):
        high = value.astype(BF16).astype(F32)
        return jnp.where(low, value - high, high)

    def columns(count, period):
        column = lax.broadcasted_iota(jnp.int32, (1, count * period), 1)
        part = jnp.zeros_like(column)
        for i in range(1, count):
            part = part + (column >= i * period).astype(jnp.int32)
        return part, column - part * period

    part, slot = columns(3, plan.z_slots)
    z_in = z_place(plan, slot, even_z)
    z_out = lax.broadcasted_iota(jnp.int32, (depth, 1), 0)
    for v in range(views):
        value = banded(v, 0, z_in - z_out - start(v, 0))
        zf_wide[v * depth : (v + 1) * depth, :] = parted(value, part == 2)
    zf_ref[...] = zf_wide[...].astype(BF16)

    column = columns(1, plan.stack)[1]
    view = jnp.zeros_like(column)
    for v in range(1, views):
        view = view + (column >= v * depth).astype(jnp.int32)
    begin = jnp.zeros_like(column)
    for v in range(views):
        begin = jnp.where(view == v, start(v, 0), begin)
    slot = lax.broadcasted_iota(jnp.int32, (plan.z_slots, 1), 0)
    delta = z_place(plan, slot, even_z) - (column - view * depth + begin)
    kernels = [kernel(v, 0) for v in range(views)]
    value = jnp.zeros(delta.shape, F32)
    for k in range(taps):
        row = jnp.zeros(column.shape, F32)
        for v in range(views):
            row = jnp.where(view == v, kernels[v][0][k] * kernels[v][1], row)
        value = jnp.where(delta == k, row, value)
    za_ref[: plan.z_slots], za_ref[plan.z_slots :] = split(value)

    def of_view(v, carry):
        slot = columns(2, plan.y_slots)[1]
        y_out = lax.broadcasted_iota(jnp.int32, (rows, 1), 0)
        high, low = split(banded(v, 1, y_place(plan, slot, even_y) - y_out - start(v, 1)))
        yf_ref[v, :rows] = high
        yf_ref[v, rows:] = low

        part, y_in = columns(3, rows)
        slot = lax.broadcasted_iota(jnp.int32, (plan.y_slots, 1), 0)
        value = banded(v, 1, y_place(plan, slot, even_y) - y_in - start(v, 1))
        ya_ref[v] = parted(value, part == 2).astype(BF16)

        x_in = lax.broadcasted_iota(jnp.int32, (lanes, lanes), 0)
        x_out = lax.broadcasted_iota(jnp.int32, (lanes, lanes), 1)
        for ref, delta in ((xf_ref, x_in - x_out), (xa_ref, x_out - x_in)):
            high, low = split(banded(v, 2, delta - start(v, 2)))
            ref[v, :, :lanes] = high
            ref[v, :, lanes:] = low
        return carry

    lax.fori_loop(0, views, of_view, 0)


SMEM = pl.BlockSpec(memory_space=pltpu.SMEM)
VMEM = pl.BlockSpec(memory_space=pltpu.VMEM)
HBM = pl.BlockSpec(memory_space=pltpu.HBM)


def call(body, operands, shapes, scalars=0, in_hbm=0, scratch=(), megabytes=24, flops=1_000):
    return pl.pallas_call(
        body,
        out_shape=[jax.ShapeDtypeStruct(*shape) for shape in shapes],
        in_specs=[SMEM] * scalars + [HBM] * in_hbm + [VMEM] * (len(operands) - scalars - in_hbm),
        out_specs=[VMEM] * len(shapes),
        scratch_shapes=list(scratch),
        compiler_params=pltpu.CompilerParams(vmem_limit_bytes=megabytes << 20),
        cost_estimate=pl.CostEstimate(flops=flops, bytes_accessed=flops, transcendentals=0),
        name=(body.func if hasattr(body, "func") else body).__name__,
    )(*operands)


def bands(plan, lengths, offsets, taps):
    views, lanes = plan.views, plan.lanes
    shapes = (
        (plan.stack, 3 * plan.z_slots),
        (2 * plan.z_slots, plan.stack),
        (views, 2 * plan.rows, 2 * plan.y_slots),
        (views, plan.y_slots, 3 * plan.rows),
        (views, lanes, 2 * lanes),
        (views, lanes, 2 * lanes),
    )
    return call(
        functools.partial(bands_kernel, plan), (lengths, offsets, taps), [(shape, BF16) for shape in shapes], in_hbm=3,
        scratch=[pltpu.VMEM(shapes[0], F32)] + [pltpu.SMEM(v.shape, v.dtype) for v in (lengths, offsets, taps)] + [pltpu.SemaphoreType.DMA((3,))],
        flops=1_000,
    )


def loop(count, body):
    unroll = max(d for d in range(1, UNROLL + 1) if count % d == 0)

    def run(i, carry):
        body(i)
        return carry

    lax.fori_loop(0, count, run, 0, unroll=unroll)


def z_forward(plan, own_ref, side_refs, zf_ref, grid_ref, pitch):
    lanes = plan.lanes

    def pair(at):
        parts = []
        for i in range(2):
            y = at * 2 + i
            pieces = [own_ref[y]] + [ref[y] for ref in side_refs]
            if plan.z_slots > plan.z_used:
                pieces.append(jnp.zeros((plan.z_slots - plan.z_used, lanes), F32))
            parts.append(three(jnp.concatenate(pieces, axis=0)))
        out = dot(zf_ref[...], jnp.concatenate(parts, axis=1))
        for i in range(2):
            grid_ref[pl.ds(at * 2 + i, plan.stack, stride=pitch), :] = out[:, i * lanes : (i + 1) * lanes]

    loop(own_ref.shape[0] // 2, pair)


def z_adjoint(plan, grid_ref, za_ref, own_out, side_outs, pitch):
    lanes, depth, side = plan.lanes, plan.depth, plan.z_side

    def pair(at):
        parts = [split(grid_ref[pl.ds(at * 2 + i, plan.stack, stride=pitch), :]) for i in range(2)]
        high, low = (jnp.concatenate(pieces, axis=1) for pieces in zip(*parts))
        both = dot(za_ref[...], high)
        out = both[: plan.z_slots] + both[plan.z_slots :] + dot(za_ref[: plan.z_slots], low)
        for i in range(2):
            value = out[:, i * lanes : (i + 1) * lanes]
            own_out[at * 2 + i] = value[:depth]
            for stage, ref in enumerate(side_outs):
                ref[at * 2 + i] = value[depth + stage * side : depth + (stage + 1) * side]

    loop(own_out.shape[0] // 2, pair)


def clear_rest(plan, grid_ref, used, padded, pitch):
    begin = used // 8 * 8
    if begin == padded:
        return
    blank = jnp.zeros((padded - begin, plan.lanes), F32)

    def one(i):
        grid_ref[pl.ds(i * pitch + begin, padded - begin), :] = blank

    loop(plan.stack, one)


def of_views(plan, field, level, yf_ref, ya_ref, xf_ref, xa_ref, views_ref, edge_ref, inner_in, inner_out):
    views, depth, rows, lanes = plan.views, plan.depth, plan.rows, plan.lanes
    edge, inner, y_slots = plan.edge_pad, plan.inner_pad, plan.y_slots

    def of_view(v, carry):
        lower, upper = field[0, v], field[1, v]
        y = lax.axis_index("view") * rows + lax.broadcasted_iota(jnp.int32, (rows, lanes), 0)
        covered = (y >= lower) & (y < upper)
        lane_forward = jnp.concatenate([xf_ref[v]] * 2, axis=0)
        lane_adjoint = jnp.concatenate([xa_ref[v]] * 2, axis=0)

        def along_x(value, matrix):
            out = dot(jnp.concatenate(split(value), axis=1), matrix)
            return out[:, :lanes] + out[:, lanes:]

        edge_base = pl.multiple_of(v * depth * plan.edge_pitch, 8)
        inner_base = pl.multiple_of(v * depth * plan.inner_pitch, 8)

        def edge_at(z):
            return pl.ds(edge_base + z * plan.edge_pitch, edge)

        def inner_at(z):
            return pl.ds(inner_base + z * plan.inner_pitch, inner)

        def slots(z):
            pieces = [edge_ref[edge_at(z), :], inner_in[inner_at(z), :]]
            if y_slots > edge + inner:
                pieces.append(jnp.zeros((y_slots - edge - inner, lanes), F32))
            return two(jnp.concatenate(pieces, axis=0))

        spread = []
        for z in range(0, depth, 2):
            parts = [slots(z + i) for i in range(2)]
            out = dot(yf_ref[v], jnp.concatenate(parts, axis=1))
            out = out[:rows] + out[rows:]
            spread += [out[:, :lanes], out[:, lanes:]]
        blurred = along_x(jnp.concatenate(spread, axis=0), lane_forward).reshape(depth, rows, lanes)
        ratio = jnp.where(covered[None], views_ref[v] / (blurred + level[v]), 1.0)
        back = along_x(ratio.reshape(depth * rows, lanes), lane_adjoint)
        for z in range(0, depth, 2):
            parts = [three(back[(z + i) * rows : (z + i + 1) * rows]) for i in range(2)]
            out = dot(ya_ref[v], jnp.concatenate(parts, axis=1))
            for i in range(2):
                edge_ref[edge_at(z + i), :] = out[:edge, i * lanes : (i + 1) * lanes]
                inner_out[inner_at(z + i), :] = out[edge : edge + inner, i * lanes : (i + 1) * lanes]
        return carry

    lax.fori_loop(0, views, of_view, 0, unroll=True)


def edges_kernel(plan, block_ref, first_ref, second_ref, inner_ref, *side_refs):
    even_z, even_y = evens()
    depth, rows, side = plan.depth, plan.rows, plan.z_side
    lasts = (even_z == 1, even_z != 1)
    for at, count, row, out_ref in (
        (0, HALO, y_first_rows(plan, even_y)[2], first_ref),
        (HALO, HALO, y_first_rows(plan, even_y)[3], second_ref),
        (2 * HALO, plan.y_inner, HALO, inner_ref),
    ):
        for i in range(count):
            value = block_ref[pl.ds(row + i, depth, stride=rows), :]
            out_ref[i] = value
            for ref, last in zip(side_refs, lasts):
                ref[at + i] = jnp.where(last, value[depth - side :], value[:side])


def grow_kernel(plan, inner_ref, zf_ref, *refs):
    side_refs, (grid_ref,) = refs[: plan.z_stages], refs[plan.z_stages :]
    clear_rest(plan, grid_ref, plan.y_inner, plan.inner_pad, plan.inner_pitch)
    z_forward(plan, inner_ref, side_refs, zf_ref, grid_ref, plan.inner_pitch)


def main_kernel(plan, inner_first, field, level, own_ref, zf_ref, za_ref, yf_ref, ya_ref, xf_ref, xa_ref, views_ref, inner_in, *refs):
    side_refs, (grid_out, own_out, *side_outs), grid_kept = refs[: plan.z_stages], refs[plan.z_stages : -1], refs[-1]
    edge_ref, inner_out = (grid_out, grid_kept) if inner_first else (grid_kept, grid_out)
    clear_rest(plan, edge_ref, plan.y_edge, plan.edge_pad, plan.edge_pitch)
    z_forward(plan, own_ref, side_refs, zf_ref, edge_ref, plan.edge_pitch)
    of_views(plan, field, level, yf_ref, ya_ref, xf_ref, xa_ref, views_ref, edge_ref, inner_in, inner_out)
    z_adjoint(plan, grid_kept, za_ref, own_out, side_outs, plan.inner_pitch if inner_first else plan.edge_pitch)


def rest_kernel(plan, pitch, grid_ref, za_ref, own_out, *side_outs):
    z_adjoint(plan, grid_ref, za_ref, own_out, side_outs, pitch)


def add_sides(plan, ref, got_refs, at, count):
    depth, side = plan.depth, plan.z_side
    even_z = evens()[0]
    value = ref[at : at + count]
    blank = jnp.zeros((count, depth - side, plan.lanes), F32)
    for got_ref, last in zip(got_refs, (even_z == 1, even_z != 1)):
        got = got_ref[at : at + count]
        value = value + jnp.where(last, jnp.concatenate([blank, got], axis=1), jnp.concatenate([got, blank], axis=1))
    return value


def sums_kernel(plan, own_halo, summed_ref, *refs):
    got_refs, (out_ref, first_ref, second_ref) = refs[: plan.z_stages], refs[plan.z_stages :]
    for i, ref in enumerate((first_ref, second_ref, first_ref, second_ref)):
        value = add_sides(plan, summed_ref, got_refs, i * HALO, HALO)
        out_ref[i * HALO : (i + 1) * HALO] = value
        if i < 2:
            ref[:HALO] = value
        elif own_halo:
            ref[HALO:] = value


def near_side(plan, value, stage):
    even_z = evens()[0]
    last = (even_z == 1, even_z != 1)[stage]
    return jnp.where(last, value[:, plan.depth - plan.z_side :], value[:, : plan.z_side])


def next_inner_kernel(plan, own_ref, summed_ref, *refs):
    got_refs, (out_ref, *side_refs) = refs[: plan.z_stages], refs[plan.z_stages :]
    for at in range(0, own_ref.shape[0], HALO + 1):
        end = min(at + HALO + 1, own_ref.shape[0])
        value = own_ref[at:end] * add_sides(plan, summed_ref, got_refs, at, end - at) * (1.0 / plan.views)
        out_ref[at:end] = value
        for stage, ref in enumerate(side_refs):
            ref[at:end] = near_side(plan, value, stage)


def next_edge_kernel(plan, own_ref, summed_ref, first_ref, second_ref, out_ref, *side_refs):
    for i, ref in enumerate((first_ref, second_ref, first_ref, second_ref)):
        a, b = i * HALO, (i + 1) * HALO
        got = ref[HALO:] if i < 2 else ref[:HALO]
        value = own_ref[a:b] * (summed_ref[a:b] + got) * (1.0 / plan.views)
        out_ref[a:b] = value
        for stage, side in enumerate(side_refs):
            side[a:b] = near_side(plan, value, stage)


def last_kernel(plan, edge_ref, inner_ref, summed_edge_ref, summed_inner_ref, first_ref, second_ref, *refs):
    got_refs, (out_ref,) = refs[: plan.z_stages], refs[plan.z_stages :]
    scale = 1.0 / plan.views
    first_row, second_row, inner_row = y_first_rows(plan, evens()[1])[2:]

    def put(row, value):
        out_ref[pl.ds(row, plan.depth, stride=plan.rows), :] = value

    for ref, row, at in ((first_ref, first_row, 2 * HALO), (second_ref, second_row, 3 * HALO)):
        for i in range(HALO):
            put(row + i, edge_ref[at + i] * (summed_edge_ref[at + i] + ref[i]) * scale)
    for i in range(inner_ref.shape[0]):
        total = add_sides(plan, summed_inner_ref, got_refs, i, 1)[0]
        put(inner_row + i, inner_ref[i] * total * scale)


def on_device(estimate, views, background, psf_taps, psf_lengths, view_offsets, field_rows):
    depth, rows, lanes = estimate.shape
    tiles, blocks = lax.axis_size("tile"), lax.axis_size("view")
    plan = Plan(views.shape[0], psf_taps.shape[2], depth, rows, lanes, tiles)
    z_pairs, y_pairs = swaps(tiles), swaps(blocks)
    side, stages, edge, inner = plan.z_side, plan.z_stages, plan.y_edge, plan.y_inner
    inner_grid = ((plan.stack * plan.inner_pitch, lanes), F32)
    edge_grid = ((plan.stack * plan.edge_pitch, lanes), F32)
    field = field_rows.T

    def own_of(count):
        return ((count, depth, lanes), F32)

    def sides_of(count):
        return [((count, side, lanes), F32)] * stages

    def run(body, operands, shapes, *static, **more):
        return call(functools.partial(body, plan, *static), operands, shapes, **more)

    def z_swap(values):
        return [lax.ppermute(value, "tile", pairs) for value, pairs in zip(values, z_pairs)]

    def y_swap(values):
        second = lax.ppermute(values[1], "view", y_pairs[1])
        return [lax.ppermute(values[0], "view", y_pairs[0]), second]

    first, second, own_inner, *sent = run(
        edges_kernel, (estimate.reshape(depth * rows, lanes),), [own_of(HALO), own_of(HALO), own_of(inner)] + sides_of(rows)
    )
    got = y_swap([first, second])
    own_side = z_swap(sent)
    zf, za, *tables = bands(plan, *[pltpu.with_memory_space_constraint(a, pltpu.HBM) for a in (psf_lengths.T, view_offsets.T, psf_taps)])
    (grown,) = run(grow_kernel, (own_inner, zf, *[value[2 * HALO :] for value in own_side]), [inner_grid])
    got, grown = lax.optimization_barrier((got, grown))
    halo = jnp.concatenate(got, axis=0)
    even_z = 1 - lax.axis_index("tile") % 2
    z_near = [jnp.where(even_z == 1, depth - side, 0), jnp.where(even_z == 1, 0, depth - side)][:stages]
    corner = z_swap([lax.dynamic_slice_in_dim(halo, at, side, 1) for at in z_near])
    edge_side = [jnp.concatenate([a, b[: 2 * HALO]], axis=0) for a, b in zip(corner, own_side)]
    own_edge = jnp.concatenate([halo, first, second], axis=0)
    for turn in range(ITERS):
        more = turn < ITERS - 1
        rows_of = {True: (inner, inner_grid), False: (edge, edge_grid)}
        (one, kept), (other, handed) = rows_of[more], rows_of[not more]
        grown, summed, *beyond = run(
            main_kernel, (field, background, own_edge, zf, za, *tables, views, grown, *edge_side),
            [handed, own_of(one)] + sides_of(one), more, scalars=2, scratch=[pltpu.VMEM(*kept)],
        )
        got_one = z_swap(beyond)
        pitch = plan.edge_pitch if more else plan.inner_pitch
        rest, *beyond = run(rest_kernel, (grown, za), [own_of(other)] + sides_of(other), pitch)
        got_one, rest, beyond = lax.optimization_barrier((got_one, rest, beyond))
        got_other = z_swap(beyond)
        (summed_inner, got_inner), (summed_edge, got_edge) = ((summed, got_one), (rest, got_other))[:: 1 if more else -1]
        sent = own_of(2 * HALO if more else HALO)
        summed_edge, *ends = run(sums_kernel, (summed_edge, *got_edge), [own_of(edge), sent, sent], more)
        got = y_swap(ends)
        if not more:
            out = run(
                last_kernel, (own_edge, own_inner, summed_edge, summed_inner, *got, *got_inner), [((depth * rows, lanes), F32)]
            )
            return out[0].reshape(depth, rows, lanes)
        own_inner, *sent = run(next_inner_kernel, (own_inner, summed_inner, *got_inner), [own_of(inner)] + sides_of(inner))
        (grown,) = run(grow_kernel, (own_inner, zf, *z_swap(sent)), [inner_grid])
        got, grown = lax.optimization_barrier((got, grown))
        own_edge, *sent = run(next_edge_kernel, (own_edge, summed_edge, *got), [own_of(edge)] + sides_of(edge))
        edge_side = z_swap(sent)


def solution(mesh):
    in_specs = (P("tile", "view", None), P(None, "tile", "view", None), P(), P(), P(), P(), P())
    out_specs = P("tile", "view", None)
    return jax.shard_map(
        on_device, mesh=mesh, in_specs=in_specs, out_specs=out_specs, check_vma=False
    )
```

```python
import functools

import jax
import jax.numpy as jnp
from jax import lax
from jax.experimental import pallas as pl
from jax.experimental.pallas import tpu as pltpu
from jax.sharding import PartitionSpec as P

ITERS = 2
HALO = 9
FAR = 1 << 20
UNROLL = 18
F32 = jnp.float32
BF16 = jnp.bfloat16


def up(size, unit):
    return -(-size // unit) * unit


def odd_tiles(count):
    return count + (8 if (count // 8) % 2 == 0 else 0)


class Plan:
    def __init__(self, views, taps, depth, rows, lanes, tiles):
        self.views, self.taps, self.depth, self.rows, self.lanes = views, taps, depth, rows, lanes
        self.z_stages = 1 if tiles == 2 else 2
        self.z_side = up(HALO, 8)
        self.z_used = depth + self.z_side * self.z_stages
        self.z_slots = up(self.z_used, 16)
        self.y_edge = 4 * HALO
        self.y_inner = rows - 2 * HALO
        self.pair_pad, self.inner_pad = up(2 * HALO, 8), up(self.y_inner, 8)
        self.y_slots = up(2 * self.pair_pad + self.inner_pad, 16)
        self.pair_pitch, self.inner_pitch = odd_tiles(self.pair_pad), odd_tiles(self.inner_pad)
        self.stack = views * depth


def swaps(count):
    first, second = [], []
    for i in range(0, count - 1, 2):
        first += [(i, i + 1), (i + 1, i)]
    for i in range(1, count - 1, 2):
        second += [(i, i + 1), (i + 1, i)]
    return first, second


def split(value):
    high = value.astype(BF16)
    return high, (value - high.astype(F32)).astype(BF16)


def two(value):
    return jnp.concatenate(split(value), axis=0)


def three(value):
    high, low = split(value)
    return jnp.concatenate([high, low, high], axis=0)


def dot(a, b):
    return jnp.dot(a, b, preferred_element_type=F32)


def z_place(plan, slot, even):
    own, side = plan.depth, plan.z_side
    after, before = slot, slot - own - side
    first = jnp.where(even == 1, after, before)
    second = jnp.where(even == 1, before - side, after - side)
    far = jnp.full_like(slot, FAR)
    last = jnp.where(slot < own + 2 * side, second, far) if plan.z_stages == 2 else far
    return jnp.where(slot < own, slot, jnp.where(slot < own + side, first, last))


def y_first_rows(plan, even):
    rows = plan.rows
    return [
        jnp.where(even == 1, rows, -HALO),
        jnp.where(even == 1, -HALO, rows),
        jnp.where(even == 1, rows - HALO, 0),
        jnp.where(even == 1, 0, rows - HALO),
        HALO,
    ]


def y_place(plan, slot, even):
    place = jnp.full_like(slot, FAR)
    pad = plan.pair_pad
    begins = [0, HALO, pad, pad + HALO, 2 * pad]
    ends = [HALO, 2 * HALO, pad + HALO, pad + 2 * HALO, 2 * pad + plan.y_inner]
    for begin, end, row in zip(begins, ends, y_first_rows(plan, even)):
        place = jnp.where((slot >= begin) & (slot < end), slot - begin + row, place)
    return place


def evens():
    return 1 - lax.axis_index("tile") % 2, 1 - lax.axis_index("view") % 2


def bands_kernel(
    plan, lengths_hbm, offsets_hbm, taps_hbm, zf_ref, za_ref, yf_ref, ya_ref, xf_ref, xa_ref, zf_wide, lengths, offsets, tap_table, sems,
):
    pairs = ((lengths_hbm, lengths), (offsets_hbm, offsets), (taps_hbm, tap_table))
    copies = [pltpu.make_async_copy(source, target, sems.at[i]) for i, (source, target) in enumerate(pairs)]
    for copy in copies:
        copy.start()
    for copy in copies:
        copy.wait()
    views, depth, rows, lanes, taps = plan.views, plan.depth, plan.rows, plan.lanes, plan.taps
    even_z, even_y = evens()

    def start(v, d):
        return offsets[d, v] - lengths[d, v] // 2

    def kernel(v, d):
        length = lengths[d, v]
        raw = [jnp.where(k < length, tap_table[v, d, k], 0.0) for k in range(taps)]
        total = raw[0]
        for one in raw[1:]:
            total = total + one
        return raw, 1.0 / jnp.full((1, lanes), total, F32)[:, :1]

    def banded(v, d, delta):
        raw, scale = kernel(v, d)
        value = jnp.zeros(delta.shape, F32)
        for k in range(taps):
            value = jnp.where(delta == k, raw[k], value)
        return value * scale

    def parted(value, low):
        high = value.astype(BF16).astype(F32)
        return jnp.where(low, value - high, high)

    def columns(count, period):
        column = lax.broadcasted_iota(jnp.int32, (1, count * period), 1)
        part = jnp.zeros_like(column)
        for i in range(1, count):
            part = part + (column >= i * period).astype(jnp.int32)
        return part, column - part * period

    part, slot = columns(3, plan.z_slots)
    z_in = z_place(plan, slot, even_z)
    z_out = lax.broadcasted_iota(jnp.int32, (depth, 1), 0)
    for v in range(views):
        value = banded(v, 0, z_in - z_out - start(v, 0))
        zf_wide[v * depth : (v + 1) * depth, :] = parted(value, part == 2)
    zf_ref[...] = zf_wide[...].astype(BF16)

    column = columns(1, plan.stack)[1]
    view = jnp.zeros_like(column)
    for v in range(1, views):
        view = view + (column >= v * depth).astype(jnp.int32)
    begin = jnp.zeros_like(column)
    for v in range(views):
        begin = jnp.where(view == v, start(v, 0), begin)
    slot = lax.broadcasted_iota(jnp.int32, (plan.z_slots, 1), 0)
    delta = z_place(plan, slot, even_z) - (column - view * depth + begin)
    kernels = [kernel(v, 0) for v in range(views)]
    value = jnp.zeros(delta.shape, F32)
    for k in range(taps):
        row = jnp.zeros(column.shape, F32)
        for v in range(views):
            row = jnp.where(view == v, kernels[v][0][k] * kernels[v][1], row)
        value = jnp.where(delta == k, row, value)
    za_ref[: plan.z_slots], za_ref[plan.z_slots :] = split(value)

    def of_view(v, carry):
        slot = columns(2, plan.y_slots)[1]
        y_out = lax.broadcasted_iota(jnp.int32, (rows, 1), 0)
        high, low = split(banded(v, 1, y_place(plan, slot, even_y) - y_out - start(v, 1)))
        yf_ref[v, :rows] = high
        yf_ref[v, rows:] = low

        part, y_in = columns(3, rows)
        slot = lax.broadcasted_iota(jnp.int32, (plan.y_slots, 1), 0)
        value = banded(v, 1, y_place(plan, slot, even_y) - y_in - start(v, 1))
        ya_ref[v] = parted(value, part == 2).astype(BF16)

        x_in = lax.broadcasted_iota(jnp.int32, (lanes, lanes), 0)
        x_out = lax.broadcasted_iota(jnp.int32, (lanes, lanes), 1)
        for ref, delta in ((xf_ref, x_in - x_out), (xa_ref, x_out - x_in)):
            high, low = split(banded(v, 2, delta - start(v, 2)))
            ref[v, :, :lanes] = high
            ref[v, :, lanes:] = low
        return carry

    lax.fori_loop(0, views, of_view, 0)


SMEM = pl.BlockSpec(memory_space=pltpu.SMEM)
VMEM = pl.BlockSpec(memory_space=pltpu.VMEM)
HBM = pl.BlockSpec(memory_space=pltpu.HBM)


def call(body, operands, shapes, scalars=0, in_hbm=0, scratch=(), megabytes=24, flops=1_000):
    return pl.pallas_call(
        body,
        out_shape=[jax.ShapeDtypeStruct(*shape) for shape in shapes],
        in_specs=[SMEM] * scalars + [HBM] * in_hbm + [VMEM] * (len(operands) - scalars - in_hbm),
        out_specs=[VMEM] * len(shapes),
        scratch_shapes=list(scratch),
        compiler_params=pltpu.CompilerParams(vmem_limit_bytes=megabytes << 20),
        cost_estimate=pl.CostEstimate(flops=flops, bytes_accessed=flops, transcendentals=0),
        name=(body.func if hasattr(body, "func") else body).__name__,
    )(*operands)


def bands(plan, lengths, offsets, taps):
    views, lanes = plan.views, plan.lanes
    shapes = (
        (plan.stack, 3 * plan.z_slots),
        (2 * plan.z_slots, plan.stack),
        (views, 2 * plan.rows, 2 * plan.y_slots),
        (views, plan.y_slots, 3 * plan.rows),
        (views, lanes, 2 * lanes),
        (views, lanes, 2 * lanes),
    )
    return call(
        functools.partial(bands_kernel, plan), (lengths, offsets, taps), [(shape, BF16) for shape in shapes], in_hbm=3,
        scratch=[pltpu.VMEM(shapes[0], F32)] + [pltpu.SMEM(v.shape, v.dtype) for v in (lengths, offsets, taps)] + [pltpu.SemaphoreType.DMA((3,))],
        flops=1_000,
    )


def loop(count, body):
    unroll = max(d for d in range(1, UNROLL + 1) if count % d == 0)

    def run(i, carry):
        body(i)
        return carry

    lax.fori_loop(0, count, run, 0, unroll=unroll)


def z_forward(plan, own_ref, side_refs, zf_ref, grid_ref, pitch, first=0, count=None):
    lanes = plan.lanes

    def pair(at):
        parts = []
        for i in range(2):
            y = first + at * 2 + i
            pieces = [own_ref[y]] + [ref[y] for ref in side_refs]
            if plan.z_slots > plan.z_used:
                pieces.append(jnp.zeros((plan.z_slots - plan.z_used, lanes), F32))
            parts.append(three(jnp.concatenate(pieces, axis=0)))
        out = dot(zf_ref[...], jnp.concatenate(parts, axis=1))
        for i in range(2):
            grid_ref[pl.ds(at * 2 + i, plan.stack, stride=pitch), :] = out[:, i * lanes : (i + 1) * lanes]

    loop((own_ref.shape[0] if count is None else count) // 2, pair)


def z_adjoint(plan, grid_ref, za_ref, own_out, side_outs, pitch, count=None, at_out=0):
    lanes, depth, side = plan.lanes, plan.depth, plan.z_side

    def pair(at):
        parts = [split(grid_ref[pl.ds(at * 2 + i, plan.stack, stride=pitch), :]) for i in range(2)]
        high, low = (jnp.concatenate(pieces, axis=1) for pieces in zip(*parts))
        both = dot(za_ref[...], high)
        out = both[: plan.z_slots] + both[plan.z_slots :] + dot(za_ref[: plan.z_slots], low)
        for i in range(2):
            value = out[:, i * lanes : (i + 1) * lanes]
            own_out[at_out + at * 2 + i] = value[:depth]
            for stage, ref in enumerate(side_outs):
                ref[at_out + at * 2 + i] = value[depth + stage * side : depth + (stage + 1) * side]

    loop((own_out.shape[0] if count is None else count) // 2, pair)


def clear_rest(plan, grid_ref, used, padded, pitch):
    begin = used // 8 * 8
    if begin == padded:
        return
    blank = jnp.zeros((padded - begin, plan.lanes), F32)

    def one(i):
        grid_ref[pl.ds(i * pitch + begin, padded - begin), :] = blank

    loop(plan.stack, one)


def of_views(plan, field, level, yf_ref, ya_ref, xf_ref, xa_ref, views_ref, grids_in, grids_out):
    views, depth, rows, lanes = plan.views, plan.depth, plan.rows, plan.lanes
    pads, y_slots = (plan.pair_pad, plan.pair_pad, plan.inner_pad), plan.y_slots
    pitches = (plan.pair_pitch, plan.pair_pitch, plan.inner_pitch)

    def of_view(v, carry):
        lower, upper = field[0, v], field[1, v]
        y = lax.axis_index("view") * rows + lax.broadcasted_iota(jnp.int32, (rows, lanes), 0)
        covered = (y >= lower) & (y < upper)
        lane_forward = jnp.concatenate([xf_ref[v]] * 2, axis=0)
        lane_adjoint = jnp.concatenate([xa_ref[v]] * 2, axis=0)

        def along_x(value, matrix):
            out = dot(jnp.concatenate(split(value), axis=1), matrix)
            return out[:, :lanes] + out[:, lanes:]

        def places(z):
            return [pl.ds((v * depth + z) * pitch, pad) for pitch, pad in zip(pitches, pads)]

        def slots(z):
            pieces = [ref[place, :] for ref, place in zip(grids_in, places(z))]
            if y_slots > sum(pads):
                pieces.append(jnp.zeros((y_slots - sum(pads), lanes), F32))
            return two(jnp.concatenate(pieces, axis=0))

        spread = []
        for z in range(0, depth, 2):
            parts = [slots(z + i) for i in range(2)]
            out = dot(yf_ref[v], jnp.concatenate(parts, axis=1))
            out = out[:rows] + out[rows:]
            spread += [out[:, :lanes], out[:, lanes:]]
        blurred = along_x(jnp.concatenate(spread, axis=0), lane_forward).reshape(depth, rows, lanes)
        ratio = jnp.where(covered[None], views_ref[v] / (blurred + level[v]), 1.0)
        back = along_x(ratio.reshape(depth * rows, lanes), lane_adjoint)
        for z in range(0, depth, 2):
            parts = [three(back[(z + i) * rows : (z + i + 1) * rows]) for i in range(2)]
            out = dot(ya_ref[v], jnp.concatenate(parts, axis=1))
            for i in range(2):
                at = 0
                for ref, place, pad in zip(grids_out, places(z + i), pads):
                    ref[place, :] = out[at : at + pad, i * lanes : (i + 1) * lanes]
                    at += pad
        return carry

    lax.fori_loop(0, views, of_view, 0, unroll=True)


def edges_kernel(plan, block_ref, first_ref, second_ref, inner_ref, *side_refs):
    even_z, even_y = evens()
    depth, rows, side = plan.depth, plan.rows, plan.z_side
    lasts = (even_z == 1, even_z != 1)
    for at, count, row, out_ref in (
        (0, HALO, y_first_rows(plan, even_y)[2], first_ref),
        (HALO, HALO, y_first_rows(plan, even_y)[3], second_ref),
        (2 * HALO, plan.y_inner, HALO, inner_ref),
    ):
        for i in range(count):
            value = block_ref[pl.ds(row + i, depth, stride=rows), :]
            out_ref[i] = value
            for ref, last in zip(side_refs, lasts):
                ref[at + i] = jnp.where(last, value[depth - side :], value[:side])


def grow_kernel(plan, inner_ref, zf_ref, *refs):
    side_refs, (grid_ref,) = refs[: plan.z_stages], refs[plan.z_stages :]
    clear_rest(plan, grid_ref, plan.y_inner, plan.inner_pad, plan.inner_pitch)
    z_forward(plan, inner_ref, side_refs, zf_ref, grid_ref, plan.inner_pitch)


def grow_near_kernel(plan, near_ref, zf_ref, *refs):
    side_refs, (grid_ref,) = refs[: plan.z_stages], refs[plan.z_stages :]
    pair_along_z(plan, near_ref, side_refs, zf_ref, grid_ref, 0)


def pair_along_z(plan, own_ref, side_refs, zf_ref, grid_ref, first):
    clear_rest(plan, grid_ref, 2 * HALO, plan.pair_pad, plan.pair_pitch)
    z_forward(plan, own_ref, side_refs, zf_ref, grid_ref, plan.pair_pitch, first, 2 * HALO)


def main_kernel(plan, field, level, halo_ref, zf_ref, za_ref, yf_ref, ya_ref, xf_ref, xa_ref, views_ref, near_in, inner_in, *refs):
    side_refs, (halo_grid, near_out, own_out, *side_outs), inner_out = refs[: plan.z_stages], refs[plan.z_stages : -1], refs[-1]
    pair_along_z(plan, halo_ref, side_refs, zf_ref, halo_grid, 0)
    grids = (halo_grid, near_in, inner_in), (halo_grid, near_out, inner_out)
    of_views(plan, field, level, yf_ref, ya_ref, xf_ref, xa_ref, views_ref, *grids)
    z_adjoint(plan, inner_out, za_ref, own_out, side_outs, plan.inner_pitch)


def last_main_kernel(plan, field, level, edge_ref, zf_ref, za_ref, yf_ref, ya_ref, xf_ref, xa_ref, views_ref, inner_in, *refs):
    side_refs, (near_grid, inner_out, own_out, *side_outs), halo_grid = refs[: plan.z_stages], refs[plan.z_stages : -1], refs[-1]
    pair_along_z(plan, edge_ref, side_refs, zf_ref, halo_grid, 0)
    pair_along_z(plan, edge_ref, side_refs, zf_ref, near_grid, 2 * HALO)
    grids = (halo_grid, near_grid, inner_in), (halo_grid, near_grid, inner_out)
    of_views(plan, field, level, yf_ref, ya_ref, xf_ref, xa_ref, views_ref, *grids)
    z_adjoint(plan, halo_grid, za_ref, own_out, side_outs, plan.pair_pitch)


def edge_rest_kernel(plan, halo_ref, near_ref, za_ref, own_out, *side_outs):
    z_adjoint(plan, halo_ref, za_ref, own_out, side_outs, plan.pair_pitch, 2 * HALO)
    z_adjoint(plan, near_ref, za_ref, own_out, side_outs, plan.pair_pitch, 2 * HALO, 2 * HALO)


def own_rest_kernel(plan, near_ref, inner_ref, za_ref, own_out, *side_outs):
    z_adjoint(plan, near_ref, za_ref, own_out, side_outs, plan.pair_pitch, 2 * HALO)
    z_adjoint(plan, inner_ref, za_ref, own_out, side_outs, plan.inner_pitch, plan.y_inner, 2 * HALO)


def add_sides(plan, ref, got_refs, at, count):
    depth, side = plan.depth, plan.z_side
    even_z = evens()[0]
    value = ref[at : at + count]
    blank = jnp.zeros((count, depth - side, plan.lanes), F32)
    for got_ref, last in zip(got_refs, (even_z == 1, even_z != 1)):
        got = got_ref[at : at + count]
        value = value + jnp.where(last, jnp.concatenate([blank, got], axis=1), jnp.concatenate([got, blank], axis=1))
    return value


def sums_kernel(plan, summed_ref, *refs):
    got_refs, (out_ref, first_ref, second_ref) = refs[: plan.z_stages], refs[plan.z_stages :]
    for i, ref in enumerate((first_ref, second_ref, first_ref, second_ref)):
        value = add_sides(plan, summed_ref, got_refs, i * HALO, HALO)
        out_ref[i * HALO : (i + 1) * HALO] = value
        at = 0 if i < 2 else HALO
        ref[at : at + HALO] = value


def last_sums_kernel(plan, summed_ref, *refs):
    got_refs, refs = refs[: plan.z_stages], refs[plan.z_stages :]
    for i, ref in enumerate(refs):
        ref[...] = add_sides(plan, summed_ref, got_refs, i * HALO, HALO)


def near_side(plan, value, stage):
    even_z = evens()[0]
    last = (even_z == 1, even_z != 1)[stage]
    return jnp.where(last, value[:, plan.depth - plan.z_side :], value[:, : plan.z_side])


def next_inner_kernel(plan, own_ref, summed_ref, *refs):
    got_refs, (out_ref, *side_refs) = refs[: plan.z_stages], refs[plan.z_stages :]
    for at in range(0, own_ref.shape[0], HALO + 1):
        end = min(at + HALO + 1, own_ref.shape[0])
        value = own_ref[at:end] * add_sides(plan, summed_ref, got_refs, at, end - at) * (1.0 / plan.views)
        out_ref[at:end] = value
        for stage, ref in enumerate(side_refs):
            ref[at:end] = near_side(plan, value, stage)


def next_edge_kernel(plan, own_ref, summed_ref, first_ref, second_ref, out_ref, *side_refs):
    for i, ref in enumerate((first_ref, second_ref, first_ref, second_ref)):
        a, b = i * HALO, (i + 1) * HALO
        got = ref[HALO:] if i < 2 else ref[:HALO]
        value = own_ref[a:b] * (summed_ref[a:b] + got) * (1.0 / plan.views)
        out_ref[a:b] = value
        for stage, side in enumerate(side_refs):
            side[a:b] = near_side(plan, value, stage)


def last_kernel(plan, edge_ref, inner_ref, summed_ref, first_ref, second_ref, *refs):
    got_refs, (out_ref,) = refs[: plan.z_stages], refs[plan.z_stages :]
    scale = 1.0 / plan.views
    first_row, second_row, inner_row = y_first_rows(plan, evens()[1])[2:]

    def put(row, value):
        out_ref[pl.ds(row, plan.depth, stride=plan.rows), :] = value

    for i in range(plan.rows):
        total = add_sides(plan, summed_ref, got_refs, i, 1)[0]
        if i < HALO:
            put(first_row + i, edge_ref[2 * HALO + i] * (total + first_ref[i]) * scale)
        elif i < 2 * HALO:
            put(second_row + i - HALO, edge_ref[2 * HALO + i] * (total + second_ref[i - HALO]) * scale)
        else:
            put(inner_row + i - 2 * HALO, inner_ref[i - 2 * HALO] * total * scale)


def on_device(estimate, views, background, psf_taps, psf_lengths, view_offsets, field_rows):
    depth, rows, lanes = estimate.shape
    tiles, blocks = lax.axis_size("tile"), lax.axis_size("view")
    plan = Plan(views.shape[0], psf_taps.shape[2], depth, rows, lanes, tiles)
    z_pairs, y_pairs = swaps(tiles), swaps(blocks)
    side, stages, edge, inner = plan.z_side, plan.z_stages, plan.y_edge, plan.y_inner
    inner_grid = ((plan.stack * plan.inner_pitch, lanes), F32)
    pair_grid = ((plan.stack * plan.pair_pitch, lanes), F32)
    field = field_rows.T

    def own_of(count):
        return ((count, depth, lanes), F32)

    def sides_of(count):
        return [((count, side, lanes), F32)] * stages

    def run(body, operands, shapes, *static, **more):
        return call(functools.partial(body, plan, *static), operands, shapes, **more)

    def z_swap(values):
        return [lax.ppermute(value, "tile", pairs) for value, pairs in zip(values, z_pairs)]

    def y_swap(values):
        second = lax.ppermute(values[1], "view", y_pairs[1])
        return [lax.ppermute(values[0], "view", y_pairs[0]), second]

    first, second, own_inner, *sent = run(
        edges_kernel, (estimate.reshape(depth * rows, lanes),), [own_of(HALO), own_of(HALO), own_of(inner)] + sides_of(rows)
    )
    got = y_swap([first, second])
    own_side = z_swap(sent)
    zf, za, *tables = bands(plan, *[pltpu.with_memory_space_constraint(a, pltpu.HBM) for a in (psf_lengths.T, view_offsets.T, psf_taps)])
    (grown,) = run(grow_kernel, (own_inner, zf, *[value[2 * HALO :] for value in own_side]), [inner_grid])
    near = jnp.concatenate([first, second], axis=0)
    (near_grown,) = run(grow_near_kernel, (near, zf, *[value[: 2 * HALO] for value in own_side]), [pair_grid])
    got, grown, near_grown = lax.optimization_barrier((got, grown, near_grown))
    halo = jnp.concatenate(got, axis=0)
    even_z = 1 - lax.axis_index("tile") % 2
    z_near = [jnp.where(even_z == 1, depth - side, 0), jnp.where(even_z == 1, 0, depth - side)][:stages]
    edge_side = z_swap([lax.dynamic_slice_in_dim(halo, at, side, 1) for at in z_near])
    own_edge = jnp.concatenate([halo, near], axis=0)
    tables = (zf, za, *tables, views)
    for turn in range(ITERS):
        if turn == ITERS - 1:
            near_grown, inner_grown, summed, *beyond = run(
                last_main_kernel, (field, background, own_edge, *tables, grown, *edge_side),
                [pair_grid, inner_grid, own_of(2 * HALO)] + sides_of(2 * HALO), scalars=2, scratch=[pltpu.VMEM(*pair_grid)],
            )
            got_halo = z_swap(beyond)
            summed_own, *beyond = run(own_rest_kernel, (near_grown, inner_grown, za), [own_of(rows)] + sides_of(rows))
            got_halo, summed_own, beyond = lax.optimization_barrier((got_halo, summed_own, beyond))
            got_own = z_swap(beyond)
            got = y_swap(run(last_sums_kernel, (summed, *got_halo), [own_of(HALO), own_of(HALO)]))
            out = run(last_kernel, (own_edge, own_inner, summed_own, *got, *got_own), [((depth * rows, lanes), F32)])
            return out[0].reshape(depth, rows, lanes)
        halo_grown, near_grown, summed_inner, *beyond = run(
            main_kernel, (field, background, halo, *tables, near_grown, grown, *edge_side),
            [pair_grid, pair_grid, own_of(inner)] + sides_of(inner), scalars=2, scratch=[pltpu.VMEM(*inner_grid)],
        )
        got_inner = z_swap(beyond)
        summed_edge, *beyond = run(edge_rest_kernel, (halo_grown, near_grown, za), [own_of(edge)] + sides_of(edge))
        got_inner, summed_edge, beyond = lax.optimization_barrier((got_inner, summed_edge, beyond))
        got_edge = z_swap(beyond)
        summed_edge, *ends = run(sums_kernel, (summed_edge, *got_edge), [own_of(edge), own_of(2 * HALO), own_of(2 * HALO)])
        got = y_swap(ends)
        own_inner, *sent = run(next_inner_kernel, (own_inner, summed_inner, *got_inner), [own_of(inner)] + sides_of(inner))
        (grown,) = run(grow_kernel, (own_inner, zf, *z_swap(sent)), [inner_grid])
        got, grown = lax.optimization_barrier((got, grown))
        own_edge, *sent = run(next_edge_kernel, (own_edge, summed_edge, *got), [own_of(edge)] + sides_of(edge))
        edge_side = z_swap(sent)


def solution(mesh):
    in_specs = (P("tile", "view", None), P(None, "tile", "view", None), P(), P(), P(), P(), P())
    out_specs = P("tile", "view", None)
    return jax.shard_map(
        on_device, mesh=mesh, in_specs=in_specs, out_specs=out_specs, check_vma=False
    )
```

```python
import functools

import jax
import jax.numpy as jnp
from jax import lax
from jax.experimental import pallas as pl
from jax.experimental.pallas import tpu as pltpu
from jax.sharding import PartitionSpec as P

ITERS = 2
HALO = 9
FAR = 1 << 20
UNROLL = 18
F32 = jnp.float32
BF16 = jnp.bfloat16


def up(size, unit):
    return -(-size // unit) * unit


def odd_tiles(count):
    return count + (8 if (count // 8) % 2 == 0 else 0)


class Plan:
    def __init__(self, views, taps, depth, rows, lanes, tiles):
        self.views, self.taps, self.depth, self.rows, self.lanes = views, taps, depth, rows, lanes
        self.z_stages = 1 if tiles == 2 else 2
        self.z_side = up(HALO, 8)
        self.z_used = depth + self.z_side * self.z_stages
        self.z_slots = up(self.z_used, 16)
        self.y_edge = 4 * HALO
        self.y_inner = rows - 2 * HALO
        self.pair_pad, self.inner_pad = up(2 * HALO, 8), up(self.y_inner, 8)
        self.y_slots = up(2 * self.pair_pad + self.inner_pad, 16)
        self.pair_pitch, self.inner_pitch = odd_tiles(self.pair_pad), odd_tiles(self.inner_pad)
        self.stack = views * depth


def swaps(count):
    first, second = [], []
    for i in range(0, count - 1, 2):
        first += [(i, i + 1), (i + 1, i)]
    for i in range(1, count - 1, 2):
        second += [(i, i + 1), (i + 1, i)]
    return first, second


def split(value):
    high = value.astype(BF16)
    return high, (value - high.astype(F32)).astype(BF16)


def two(value):
    return jnp.concatenate(split(value), axis=0)


def three(value):
    high, low = split(value)
    return jnp.concatenate([high, low, high], axis=0)


def dot(a, b):
    return jnp.dot(a, b, preferred_element_type=F32)


def z_place(plan, slot, even):
    own, side = plan.depth, plan.z_side
    after, before = slot, slot - own - side
    first = jnp.where(even == 1, after, before)
    second = jnp.where(even == 1, before - side, after - side)
    far = jnp.full_like(slot, FAR)
    last = jnp.where(slot < own + 2 * side, second, far) if plan.z_stages == 2 else far
    return jnp.where(slot < own, slot, jnp.where(slot < own + side, first, last))


def y_first_rows(plan, even):
    rows = plan.rows
    return [
        jnp.where(even == 1, rows, -HALO),
        jnp.where(even == 1, -HALO, rows),
        jnp.where(even == 1, rows - HALO, 0),
        jnp.where(even == 1, 0, rows - HALO),
        HALO,
    ]


def y_place(plan, slot, even):
    place = jnp.full_like(slot, FAR)
    pad = plan.pair_pad
    begins = [0, HALO, pad, pad + HALO, 2 * pad]
    ends = [HALO, 2 * HALO, pad + HALO, pad + 2 * HALO, 2 * pad + plan.y_inner]
    for begin, end, row in zip(begins, ends, y_first_rows(plan, even)):
        place = jnp.where((slot >= begin) & (slot < end), slot - begin + row, place)
    return place


def evens():
    return 1 - lax.axis_index("tile") % 2, 1 - lax.axis_index("view") % 2


def bands_kernel(
    plan, lengths_hbm, offsets_hbm, taps_hbm, zf_ref, za_ref, yf_ref, ya_ref, xf_ref, xa_ref, zf_wide, lengths, offsets, tap_table, sems,
):
    pairs = ((lengths_hbm, lengths), (offsets_hbm, offsets), (taps_hbm, tap_table))
    copies = [pltpu.make_async_copy(source, target, sems.at[i]) for i, (source, target) in enumerate(pairs)]
    for copy in copies:
        copy.start()
    for copy in copies:
        copy.wait()
    views, depth, rows, lanes, taps = plan.views, plan.depth, plan.rows, plan.lanes, plan.taps
    even_z, even_y = evens()

    def start(v, d):
        return offsets[d, v] - lengths[d, v] // 2

    def kernel(v, d):
        length = lengths[d, v]
        raw = [jnp.where(k < length, tap_table[v, d, k], 0.0) for k in range(taps)]
        total = raw[0]
        for one in raw[1:]:
            total = total + one
        return raw, 1.0 / jnp.full((1, lanes), total, F32)[:, :1]

    def banded(v, d, delta):
        raw, scale = kernel(v, d)
        value = jnp.zeros(delta.shape, F32)
        for k in range(taps):
            value = jnp.where(delta == k, raw[k], value)
        return value * scale

    def parted(value, low):
        high = value.astype(BF16).astype(F32)
        return jnp.where(low, value - high, high)

    def columns(count, period):
        column = lax.broadcasted_iota(jnp.int32, (1, count * period), 1)
        part = jnp.zeros_like(column)
        for i in range(1, count):
            part = part + (column >= i * period).astype(jnp.int32)
        return part, column - part * period

    part, slot = columns(3, plan.z_slots)
    z_in = z_place(plan, slot, even_z)
    z_out = lax.broadcasted_iota(jnp.int32, (depth, 1), 0)
    for v in range(views):
        value = banded(v, 0, z_in - z_out - start(v, 0))
        zf_wide[v * depth : (v + 1) * depth, :] = parted(value, part == 2)
    zf_ref[...] = zf_wide[...].astype(BF16)

    column = columns(1, plan.stack)[1]
    view = jnp.zeros_like(column)
    for v in range(1, views):
        view = view + (column >= v * depth).astype(jnp.int32)
    begin = jnp.zeros_like(column)
    for v in range(views):
        begin = jnp.where(view == v, start(v, 0), begin)
    slot = lax.broadcasted_iota(jnp.int32, (plan.z_slots, 1), 0)
    delta = z_place(plan, slot, even_z) - (column - view * depth + begin)
    kernels = [kernel(v, 0) for v in range(views)]
    value = jnp.zeros(delta.shape, F32)
    for k in range(taps):
        row = jnp.zeros(column.shape, F32)
        for v in range(views):
            row = jnp.where(view == v, kernels[v][0][k] * kernels[v][1], row)
        value = jnp.where(delta == k, row, value)
    za_ref[: plan.z_slots], za_ref[plan.z_slots :] = split(value)

    def of_view(v, carry):
        slot = columns(2, plan.y_slots)[1]
        y_out = lax.broadcasted_iota(jnp.int32, (rows, 1), 0)
        high, low = split(banded(v, 1, y_place(plan, slot, even_y) - y_out - start(v, 1)))
        yf_ref[v, :rows] = high
        yf_ref[v, rows:] = low

        part, y_in = columns(3, rows)
        slot = lax.broadcasted_iota(jnp.int32, (plan.y_slots, 1), 0)
        value = banded(v, 1, y_place(plan, slot, even_y) - y_in - start(v, 1))
        ya_ref[v] = parted(value, part == 2).astype(BF16)

        x_in = lax.broadcasted_iota(jnp.int32, (lanes, lanes), 0)
        x_out = lax.broadcasted_iota(jnp.int32, (lanes, lanes), 1)
        for ref, delta in ((xf_ref, x_in - x_out), (xa_ref, x_out - x_in)):
            high, low = split(banded(v, 2, delta - start(v, 2)))
            ref[v, :, :lanes] = high
            ref[v, :, lanes:] = low
        return carry

    lax.fori_loop(0, views, of_view, 0)


SMEM = pl.BlockSpec(memory_space=pltpu.SMEM)
VMEM = pl.BlockSpec(memory_space=pltpu.VMEM)
HBM = pl.BlockSpec(memory_space=pltpu.HBM)


def call(body, operands, shapes, scalars=0, in_hbm=0, scratch=(), megabytes=24, flops=1_000):
    return pl.pallas_call(
        body,
        out_shape=[jax.ShapeDtypeStruct(*shape) for shape in shapes],
        in_specs=[SMEM] * scalars + [HBM] * in_hbm + [VMEM] * (len(operands) - scalars - in_hbm),
        out_specs=[VMEM] * len(shapes),
        scratch_shapes=list(scratch),
        compiler_params=pltpu.CompilerParams(vmem_limit_bytes=megabytes << 20),
        cost_estimate=pl.CostEstimate(flops=flops, bytes_accessed=flops, transcendentals=0),
        name=(body.func if hasattr(body, "func") else body).__name__,
    )(*operands)


def bands(plan, lengths, offsets, taps):
    views, lanes = plan.views, plan.lanes
    shapes = (
        (plan.stack, 3 * plan.z_slots),
        (2 * plan.z_slots, plan.stack),
        (views, 2 * plan.rows, 2 * plan.y_slots),
        (views, plan.y_slots, 3 * plan.rows),
        (views, lanes, 2 * lanes),
        (views, lanes, 2 * lanes),
    )
    return call(
        functools.partial(bands_kernel, plan), (lengths, offsets, taps), [(shape, BF16) for shape in shapes], in_hbm=3,
        scratch=[pltpu.VMEM(shapes[0], F32)] + [pltpu.SMEM(v.shape, v.dtype) for v in (lengths, offsets, taps)] + [pltpu.SemaphoreType.DMA((3,))],
        flops=1_000,
    )


def loop(count, body):
    unroll = max(d for d in range(1, UNROLL + 1) if count % d == 0)

    def run(i, carry):
        body(i)
        return carry

    lax.fori_loop(0, count, run, 0, unroll=unroll)


def z_forward(plan, own_ref, side_refs, zf_ref, grid_ref, pitch, first=0, count=None):
    lanes = plan.lanes

    def pair(at):
        parts = []
        for i in range(2):
            y = first + at * 2 + i
            pieces = [own_ref[y]] + [ref[y] for ref in side_refs]
            if plan.z_slots > plan.z_used:
                pieces.append(jnp.zeros((plan.z_slots - plan.z_used, lanes), F32))
            parts.append(three(jnp.concatenate(pieces, axis=0)))
        out = dot(zf_ref[...], jnp.concatenate(parts, axis=1))
        for i in range(2):
            grid_ref[pl.ds(at * 2 + i, plan.stack, stride=pitch), :] = out[:, i * lanes : (i + 1) * lanes]

    loop((own_ref.shape[0] if count is None else count) // 2, pair)


def z_adjoint(plan, grid_ref, za_ref, own_out, side_outs, pitch, count=None, at_out=0, with_near=False):
    lanes, depth, side = plan.lanes, plan.depth, plan.z_side

    def pair(at):
        parts = [split(grid_ref[pl.ds(at * 2 + i, plan.stack, stride=pitch), :]) for i in range(2)]
        high, low = (jnp.concatenate(pieces, axis=1) for pieces in zip(*parts))
        both = dot(za_ref[...], high)
        out = both[: plan.z_slots] + both[plan.z_slots :] + dot(za_ref[: plan.z_slots], low)
        for i in range(2):
            value = out[:, i * lanes : (i + 1) * lanes]
            own_out[at_out + at * 2 + i] = value[:depth]
            for stage, ref in enumerate(side_outs):
                sent = value[depth + stage * side : depth + (stage + 1) * side]
                if with_near:
                    sent = jnp.concatenate([sent, near_side(plan, value[:depth], stage)], axis=0)
                ref[at_out + at * 2 + i] = sent

    loop((own_out.shape[0] if count is None else count) // 2, pair)


def clear_rest(plan, grid_ref, used, padded, pitch):
    begin = used // 8 * 8
    if begin == padded:
        return
    blank = jnp.zeros((padded - begin, plan.lanes), F32)

    def one(i):
        grid_ref[pl.ds(i * pitch + begin, padded - begin), :] = blank

    loop(plan.stack, one)


def of_views(plan, field, level, yf_ref, ya_ref, xf_ref, xa_ref, views_ref, grids_in, grids_out):
    views, depth, rows, lanes = plan.views, plan.depth, plan.rows, plan.lanes
    pads, y_slots = (plan.pair_pad, plan.pair_pad, plan.inner_pad), plan.y_slots
    pitches = (plan.pair_pitch, plan.pair_pitch, plan.inner_pitch)

    def of_view(v, carry):
        lower, upper = field[0, v], field[1, v]
        y = lax.axis_index("view") * rows + lax.broadcasted_iota(jnp.int32, (rows, lanes), 0)
        covered = (y >= lower) & (y < upper)
        lane_forward = jnp.concatenate([xf_ref[v]] * 2, axis=0)
        lane_adjoint = jnp.concatenate([xa_ref[v]] * 2, axis=0)

        def along_x(value, matrix):
            out = dot(jnp.concatenate(split(value), axis=1), matrix)
            return out[:, :lanes] + out[:, lanes:]

        def places(z):
            return [pl.ds((v * depth + z) * pitch, pad) for pitch, pad in zip(pitches, pads)]

        def slots(z):
            pieces = [ref[place, :] for ref, place in zip(grids_in, places(z))]
            if y_slots > sum(pads):
                pieces.append(jnp.zeros((y_slots - sum(pads), lanes), F32))
            return two(jnp.concatenate(pieces, axis=0))

        spread = []
        for z in range(0, depth, 2):
            parts = [slots(z + i) for i in range(2)]
            out = dot(yf_ref[v], jnp.concatenate(parts, axis=1))
            out = out[:rows] + out[rows:]
            spread += [out[:, :lanes], out[:, lanes:]]
        blurred = along_x(jnp.concatenate(spread, axis=0), lane_forward).reshape(depth, rows, lanes)
        ratio = jnp.where(covered[None], views_ref[v] / (blurred + level[v]), 1.0)
        back = along_x(ratio.reshape(depth * rows, lanes), lane_adjoint)
        for z in range(0, depth, 2):
            parts = [three(back[(z + i) * rows : (z + i + 1) * rows]) for i in range(2)]
            out = dot(ya_ref[v], jnp.concatenate(parts, axis=1))
            for i in range(2):
                at = 0
                for ref, place, pad in zip(grids_out, places(z + i), pads):
                    ref[place, :] = out[at : at + pad, i * lanes : (i + 1) * lanes]
                    at += pad
        return carry

    lax.fori_loop(0, views, of_view, 0, unroll=True)


def edges_kernel(plan, block_ref, first_ref, second_ref, inner_ref, *side_refs):
    even_z, even_y = evens()
    depth, rows, side = plan.depth, plan.rows, plan.z_side
    lasts = (even_z == 1, even_z != 1)
    for at, count, row, out_ref in (
        (0, HALO, y_first_rows(plan, even_y)[2], first_ref),
        (HALO, HALO, y_first_rows(plan, even_y)[3], second_ref),
        (2 * HALO, plan.y_inner, HALO, inner_ref),
    ):
        for i in range(count):
            value = block_ref[pl.ds(row + i, depth, stride=rows), :]
            out_ref[i] = value
            for ref, last in zip(side_refs, lasts):
                ref[at + i] = jnp.where(last, value[depth - side :], value[:side])


def grow_kernel(plan, inner_ref, zf_ref, *refs):
    side_refs, (grid_ref,) = refs[: plan.z_stages], refs[plan.z_stages :]
    clear_rest(plan, grid_ref, plan.y_inner, plan.inner_pad, plan.inner_pitch)
    z_forward(plan, inner_ref, side_refs, zf_ref, grid_ref, plan.inner_pitch)


def grow_near_kernel(plan, near_ref, zf_ref, *refs):
    side_refs, (grid_ref,) = refs[: plan.z_stages], refs[plan.z_stages :]
    pair_along_z(plan, near_ref, side_refs, zf_ref, grid_ref, 0)


def pair_along_z(plan, own_ref, side_refs, zf_ref, grid_ref, first):
    clear_rest(plan, grid_ref, 2 * HALO, plan.pair_pad, plan.pair_pitch)
    z_forward(plan, own_ref, side_refs, zf_ref, grid_ref, plan.pair_pitch, first, 2 * HALO)


def main_kernel(plan, field, level, halo_ref, zf_ref, za_ref, yf_ref, ya_ref, xf_ref, xa_ref, views_ref, near_in, inner_in, *refs):
    side_refs, refs = refs[: plan.z_stages], refs[plan.z_stages :]
    (inner_out, own_out, *side_outs), (halo_grid, near_out) = refs[:-2], refs[-2:]
    pair_along_z(plan, halo_ref, side_refs, zf_ref, halo_grid, 0)
    grids = (halo_grid, near_in, inner_in), (halo_grid, near_out, inner_out)
    of_views(plan, field, level, yf_ref, ya_ref, xf_ref, xa_ref, views_ref, *grids)
    z_adjoint(plan, halo_grid, za_ref, own_out, side_outs, plan.pair_pitch, 2 * HALO)
    z_adjoint(plan, near_out, za_ref, own_out, side_outs, plan.pair_pitch, 2 * HALO, 2 * HALO)


def last_main_kernel(plan, field, level, edge_ref, zf_ref, za_ref, yf_ref, ya_ref, xf_ref, xa_ref, views_ref, inner_in, *refs):
    side_refs, (near_grid, inner_out, own_out, *side_outs), halo_grid = refs[: plan.z_stages], refs[plan.z_stages : -1], refs[-1]
    pair_along_z(plan, edge_ref, side_refs, zf_ref, halo_grid, 0)
    pair_along_z(plan, edge_ref, side_refs, zf_ref, near_grid, 2 * HALO)
    grids = (halo_grid, near_grid, inner_in), (halo_grid, near_grid, inner_out)
    of_views(plan, field, level, yf_ref, ya_ref, xf_ref, xa_ref, views_ref, *grids)
    z_adjoint(plan, halo_grid, za_ref, own_out, side_outs, plan.pair_pitch)


def inner_rest_kernel(plan, inner_ref, za_ref, own_out, *side_outs):
    z_adjoint(plan, inner_ref, za_ref, own_out, side_outs, plan.inner_pitch, with_near=True)


def own_rest_kernel(plan, near_ref, inner_ref, za_ref, own_out, *side_outs):
    z_adjoint(plan, near_ref, za_ref, own_out, side_outs, plan.pair_pitch, 2 * HALO)
    z_adjoint(plan, inner_ref, za_ref, own_out, side_outs, plan.inner_pitch, plan.y_inner, 2 * HALO)


def add_sides(plan, ref, got_refs, at, count):
    depth, side = plan.depth, plan.z_side
    even_z = evens()[0]
    value = ref[at : at + count]
    blank = jnp.zeros((count, depth - side, plan.lanes), F32)
    for got_ref, last in zip(got_refs, (even_z == 1, even_z != 1)):
        got = got_ref[at : at + count, : plan.z_side]
        value = value + jnp.where(last, jnp.concatenate([blank, got], axis=1), jnp.concatenate([got, blank], axis=1))
    return value


def sums_kernel(plan, summed_ref, *refs):
    got_refs, (out_ref, first_ref, second_ref) = refs[: plan.z_stages], refs[plan.z_stages :]
    for i, ref in enumerate((first_ref, second_ref, first_ref, second_ref)):
        value = add_sides(plan, summed_ref, got_refs, i * HALO, HALO)
        out_ref[i * HALO : (i + 1) * HALO] = value
        at = 0 if i < 2 else HALO
        ref[at : at + HALO] = value


def last_sums_kernel(plan, summed_ref, *refs):
    got_refs, refs = refs[: plan.z_stages], refs[plan.z_stages :]
    for i, ref in enumerate(refs):
        ref[...] = add_sides(plan, summed_ref, got_refs, i * HALO, HALO)


def near_side(plan, value, stage):
    even_z = evens()[0]
    last = (even_z == 1, even_z != 1)[stage]
    return jnp.where(last, value[..., plan.depth - plan.z_side :, :], value[..., : plan.z_side, :])


def next_inner_kernel(plan, own_ref, summed_ref, *refs):
    stages, side, scale = plan.z_stages, plan.z_side, 1.0 / plan.views
    side_refs, beyond_refs, got_refs, (out_ref, *side_outs) = [refs[i * stages : (i + 1) * stages] for i in range(3)] + [refs[3 * stages :]]
    for at in range(0, own_ref.shape[0], HALO + 1):
        end = min(at + HALO + 1, own_ref.shape[0])
        out_ref[at:end] = own_ref[at:end] * add_sides(plan, summed_ref, got_refs, at, end - at) * scale
        for old, mine, theirs, new in zip(side_refs, beyond_refs, got_refs, side_outs):
            new[at:end] = old[at:end] * (mine[at:end, :side] + theirs[at:end, side:]) * scale


def next_edge_kernel(plan, own_ref, summed_ref, first_ref, second_ref, out_ref, *side_refs):
    for i, ref in enumerate((first_ref, second_ref, first_ref, second_ref)):
        a, b = i * HALO, (i + 1) * HALO
        got = ref[HALO:] if i < 2 else ref[:HALO]
        value = own_ref[a:b] * (summed_ref[a:b] + got) * (1.0 / plan.views)
        out_ref[a:b] = value
        for stage, side in enumerate(side_refs):
            side[a:b] = near_side(plan, value, stage)


def last_kernel(plan, edge_ref, inner_ref, summed_ref, first_ref, second_ref, *refs):
    got_refs, (out_ref, turned_ref) = refs[: plan.z_stages], refs[plan.z_stages :]
    scale = 1.0 / plan.views
    first_row, second_row, inner_row = y_first_rows(plan, evens()[1])[2:]

    def put(row, value):
        turned_ref[pl.ds(row, plan.depth, stride=odd_tiles(plan.rows)), :] = value

    for i in range(plan.rows):
        total = add_sides(plan, summed_ref, got_refs, i, 1)[0]
        if i < HALO:
            put(first_row + i, edge_ref[2 * HALO + i] * (total + first_ref[i]) * scale)
        elif i < 2 * HALO:
            put(second_row + i - HALO, edge_ref[2 * HALO + i] * (total + second_ref[i - HALO]) * scale)
        else:
            put(inner_row + i - 2 * HALO, inner_ref[i - 2 * HALO] * total * scale)
    for z in range(plan.depth):
        out_ref[z * plan.rows : (z + 1) * plan.rows] = turned_ref[pl.ds(z * odd_tiles(plan.rows), plan.rows), :]


def on_device(estimate, views, background, psf_taps, psf_lengths, view_offsets, field_rows):
    depth, rows, lanes = estimate.shape
    tiles, blocks = lax.axis_size("tile"), lax.axis_size("view")
    plan = Plan(views.shape[0], psf_taps.shape[2], depth, rows, lanes, tiles)
    z_pairs, y_pairs = swaps(tiles), swaps(blocks)
    side, stages, edge, inner = plan.z_side, plan.z_stages, plan.y_edge, plan.y_inner
    inner_grid = ((plan.stack * plan.inner_pitch, lanes), F32)
    pair_grid = ((plan.stack * plan.pair_pitch, lanes), F32)
    field = field_rows.T

    def own_of(count):
        return ((count, depth, lanes), F32)

    def sides_of(count):
        return [((count, side, lanes), F32)] * stages

    def run(body, operands, shapes, *static, **more):
        return call(functools.partial(body, plan, *static), operands, shapes, **more)

    def z_swap(values):
        return [lax.ppermute(value, "tile", pairs) for value, pairs in zip(values, z_pairs)]

    def y_swap(values):
        second = lax.ppermute(values[1], "view", y_pairs[1])
        return [lax.ppermute(values[0], "view", y_pairs[0]), second]

    first, second, own_inner, *sent = run(
        edges_kernel, (estimate.reshape(depth * rows, lanes),), [own_of(HALO), own_of(HALO), own_of(inner)] + sides_of(rows)
    )
    got = y_swap([first, second])
    own_side = z_swap(sent)
    zf, za, *tables = bands(plan, *[pltpu.with_memory_space_constraint(a, pltpu.HBM) for a in (psf_lengths.T, view_offsets.T, psf_taps)])
    inner_side = [value[2 * HALO :] for value in own_side]
    (grown,) = run(grow_kernel, (own_inner, zf, *inner_side), [inner_grid])
    near = jnp.concatenate([first, second], axis=0)
    (near_grown,) = run(grow_near_kernel, (near, zf, *[value[: 2 * HALO] for value in own_side]), [pair_grid])
    got, grown, near_grown = lax.optimization_barrier((got, grown, near_grown))
    halo = jnp.concatenate(got, axis=0)
    even_z = 1 - lax.axis_index("tile") % 2
    z_near = [jnp.where(even_z == 1, depth - side, 0), jnp.where(even_z == 1, 0, depth - side)][:stages]
    edge_side = z_swap([lax.dynamic_slice_in_dim(halo, at, side, 1) for at in z_near])
    own_edge = jnp.concatenate([halo, near], axis=0)
    tables = (zf, za, *tables, views)
    for turn in range(ITERS):
        if turn == ITERS - 1:
            near_grown, inner_grown, summed, *beyond = run(
                last_main_kernel, (field, background, own_edge, *tables, grown, *edge_side),
                [pair_grid, inner_grid, own_of(2 * HALO)] + sides_of(2 * HALO), scalars=2, scratch=[pltpu.VMEM(*pair_grid)],
            )
            got_halo = z_swap(beyond)
            summed_own, *beyond = run(own_rest_kernel, (near_grown, inner_grown, za), [own_of(rows)] + sides_of(rows))
            got_halo, summed_own, beyond = lax.optimization_barrier((got_halo, summed_own, beyond))
            got_own = z_swap(beyond)
            got = y_swap(run(last_sums_kernel, (summed, *got_halo), [own_of(HALO), own_of(HALO)]))
            out = run(
                last_kernel, (own_edge, own_inner, summed_own, *got, *got_own), [((depth * rows, lanes), F32)],
                scratch=[pltpu.VMEM((depth * odd_tiles(rows), lanes), F32)],
            )
            return out[0].reshape(depth, rows, lanes)
        inner_grown, summed_edge, *beyond = run(
            main_kernel, (field, background, halo, *tables, near_grown, grown, *edge_side),
            [inner_grid, own_of(edge)] + sides_of(edge), scalars=2, scratch=[pltpu.VMEM(*pair_grid)] * 2,
        )
        got_edge = z_swap(beyond)
        both = [((inner, 2 * side, lanes), F32)] * stages
        summed_inner, *beyond = run(inner_rest_kernel, (inner_grown, za), [own_of(inner)] + both)
        got_edge, summed_inner, beyond = lax.optimization_barrier((got_edge, summed_inner, beyond))
        got_inner = z_swap(beyond)
        summed_edge, *ends = run(sums_kernel, (summed_edge, *got_edge), [own_of(edge), own_of(2 * HALO), own_of(2 * HALO)])
        got = y_swap(ends)
        got, got_inner = lax.optimization_barrier((got, got_inner))
        own_edge, *sent = run(next_edge_kernel, (own_edge, summed_edge, *got), [own_of(edge)] + sides_of(edge))
        edge_side = z_swap(sent)
        own_inner, *inner_side = run(
            next_inner_kernel, (own_inner, summed_inner, *inner_side, *beyond, *got_inner), [own_of(inner)] + sides_of(inner)
        )
        (grown,) = run(grow_kernel, (own_inner, zf, *inner_side), [inner_grid])


def solution(mesh):
    in_specs = (P("tile", "view", None), P(None, "tile", "view", None), P(), P(), P(), P(), P())
    out_specs = P("tile", "view", None)
    return jax.shard_map(
        on_device, mesh=mesh, in_specs=in_specs, out_specs=out_specs, check_vma=False
    )
```
